256 devices in a mesh: ctx: 32 (over y, z), head: 8 (over x, core).
Axes of the slice: x: 4, y: 4, z: 8, core: 2. Of those that a mesh axis runs over, the one named last changes fastest.
Arguments:
- queries: bfloat16 [32768, 2048], P('ctx', 'head'), may hold values from -6 to 6
- key_vectors: bfloat16 [32768, 2048], P('ctx', 'head'), may hold values from -6 to 6
- value_vectors: bfloat16 [32768, 2048], P('ctx', 'head'), may hold values from -60 to 60
- write_rates: float32 [32768, 16], P('ctx', 'head'), may hold values from 0 to 1
- doc_lengths: int32 [32], replicated, may hold values from 1 to 16384, 32768 in all
- norm_gain: float32 [2048], P('head'), may hold values from 0.5 to 1.5
Outputs:
- normed: bfloat16 [32768, 2048], P('ctx', 'head')
The draws below stay inside these ranges and needn't reach their ends.
All inputs are finite; a program needn't handle non-finite values.
Results may differ from the reference program's by a relative error of at most 0.0014.
Values sent between devices are 32-bit elements; how exact they have to be, the bound alone decides.
A program may use at most 64 MiB of HBM per device.

```python
import math
import jax
import jax.numpy as jnp
import numpy as np
from jax import lax

HEAD_DIM = 128
TOK_DEV = 1024
NDOCS = 32
HEADS = 16
WIDTH = 2048
SEQ_SLOTS = 32768


def draw_value_vectors(key, part):
    root_seed_handle, key_rows = jax.random.split(key, 2)
    columns = jnp.arange(WIDTH)
    head_of = (columns // HEAD_DIM).astype(jnp.float32)
    ramp = 0.5 * 3.0 ** (head_of / max(HEADS - 1, 1))
    row_scale = jnp.exp(jax.random.uniform(key_rows, (SEQ_SLOTS, 1), minval=0.0, maxval=math.log(10.0))) / 3.0
    base = jnp.clip(jax.random.normal(root_seed_handle, (SEQ_SLOTS, WIDTH)), -5.0, 5.0)
    return (base * row_scale * ramp[None, :]).astype(jnp.bfloat16)


def draw_write_rates(key, part):
    root_seed_handle = jax.random.fold_in(key, 1)
    accelerator_seed_handle = jax.random.fold_in(key, 2)
    element_seed_handle = jax.random.fold_in(key, 3)
    cluster_seed_handle = jax.random.fold_in(key, 4)
    low = min(1.0, 2.0 * HEAD_DIM / SEQ_SLOTS)
    spread = jnp.exp(jax.random.uniform(root_seed_handle, (HEADS,), minval=math.log(low), maxval=0.0))
    base = spread
    device_factor = jnp.exp(jax.random.uniform(accelerator_seed_handle, (SEQ_SLOTS // TOK_DEV, 1, HEADS), minval=math.log(0.5), maxval=0.0))
    device_factor = jnp.broadcast_to(device_factor, (SEQ_SLOTS // TOK_DEV, TOK_DEV, HEADS)).reshape(SEQ_SLOTS, HEADS)
    token_factor = jax.random.uniform(element_seed_handle, (SEQ_SLOTS, HEADS), minval=0.5, maxval=1.0)
    rates = jnp.minimum(base[None, :] * device_factor * token_factor, 1.0)
    cluster_bunches = jax.random.randint(cluster_seed_handle, (8,), 0, SEQ_SLOTS)
    agreement_indicator = jnp.any(jnp.arange(SEQ_SLOTS)[:, None] == cluster_bunches[None, :], axis=1)
    return jnp.where(agreement_indicator[:, None], 1.0, rates).astype(jnp.float32)


def block_scale(own_key, extent, shards, smallest, high):
    def one(position, shards_of):
        steps = jax.random.uniform(jax.random.fold_in(jax.random.fold_in(own_key, 6), position), (shards_of,), jnp.float32, smallest / len(shards), high / len(shards))
        return jnp.repeat(jnp.exp(steps), extent[position] // shards_of).reshape((-1,) + (1,) * (len(extent) - position - 1))

    factor_of = one(*shards[0])
    for cut in shards[1:]:
        factor_of = factor_of * one(*cut)
    return factor_of


def split_up(count, total, reach, lean):
    portions = [(1 << 20) // math.isqrt(rank ** lean) + 1 for rank in range(2, count + 1)]
    spare, counts = total - reach - (count - 1), [1] * (count - 1)
    while spare > 0:
        candidates = [i for i in range(count - 1) if counts[i] < reach]
        pool, budget = sum([portions[i] for i in candidates]), spare
        for i in candidates:
            more = min(reach - counts[i], max(1, budget * portions[i] // pool), spare)
            counts[i] = counts[i] + more
            spare = spare - more
    return np.array([reach] + counts)


def uneven_parts(own_key, amount, total, most, slope):
    if amount == 2:
        one = jax.random.randint(own_key, (), max(1, total - most), min(most, total - 1) + 1)
        return jnp.stack([one, total - one])
    sizes = jnp.asarray(split_up(amount, total, most, slope), jnp.int32)
    pairs = (amount - 1) // 2
    source_of, receiver = sizes[1:1 + 2 * pairs:2], sizes[2:2 + 2 * pairs:2]
    margin = jnp.minimum(source_of - 1, most - receiver)
    moved = jax.random.randint(jax.random.fold_in(own_key, 1), (pairs,), 0, 1 << 20) % (margin + 1)
    sizes = sizes.at[1:1 + 2 * pairs:2].set(source_of - moved).at[2:2 + 2 * pairs:2].set(receiver + moved)
    return sizes[jax.random.permutation(jax.random.fold_in(own_key, 2), amount)]


def gaussian(own_key, shape, scale, most, shards=(), kind=jnp.bfloat16):
    drawn = jax.random.normal(own_key, shape, jnp.float32) * scale
    if len(shards) > 0:
        drawn = block_scale(own_key, shape, shards, -0.22, 0.18) * drawn
    return jnp.clip(drawn, min=-most, max=most).astype(kind)


def setup_inputs(seed: int = 0) -> dict:
    key_of = jax.random.split(jax.random.key(seed), 7)
    queries = gaussian(key_of[0], (SEQ_SLOTS, WIDTH), 1.0, 6.0, ((0, 32), (1, 8)))
    key_vectors = gaussian(key_of[1], (SEQ_SLOTS, WIDTH), 1.0, 6.0, ((0, 32), (1, 8)))
    value_vectors = draw_value_vectors(jax.random.fold_in(key_of[6], 71), 0)
    write_rates = draw_write_rates(jax.random.fold_in(key_of[6], 71), 0)
    doc_lengths = uneven_parts(key_of[4], NDOCS, SEQ_SLOTS, SEQ_SLOTS // 2, 2).astype(jnp.int32)
    norm_gain = jnp.clip(1.0 + 0.1 * jax.random.normal(key_of[5], (WIDTH,), jnp.float32), 0.5, 1.5)
    return dict(queries=queries, key_vectors=key_vectors, value_vectors=value_vectors, write_rates=write_rates, doc_lengths=doc_lengths, norm_gain=norm_gain)


highest = lax.Precision.HIGHEST

def normalize(rows):
    return rows * lax.rsqrt(lax.optimization_barrier(jnp.sum(rows * rows, axis=-1, keepdims=True)) + 1e-06)

def reference(queries, key_vectors, value_vectors, write_rates, doc_lengths, norm_gain):
    query_rows = normalize(queries.astype(jnp.float32).reshape(SEQ_SLOTS, HEADS, HEAD_DIM))
    key_rows = normalize(key_vectors.astype(jnp.float32).reshape(SEQ_SLOTS, HEADS, HEAD_DIM))
    value_rows = value_vectors.astype(jnp.float32).reshape(SEQ_SLOTS, HEADS, HEAD_DIM)
    ends = jnp.cumsum(doc_lengths, dtype=jnp.int32)
    begins = ends - doc_lengths
    positions = jnp.arange(SEQ_SLOTS, dtype=jnp.int32)
    is_start = jnp.any(begins[None, :] == positions[:, None], axis=1)

    def advance(state, inputs):
        query_now, key_now, value_now, rate_now, start_now = inputs
        state = jnp.where(start_now, jnp.zeros_like(state), state)
        recalled = jnp.einsum('hde,hd->he', state, key_now, precision=highest)
        state = state + rate_now[:, None, None] * key_now[:, :, None] * (value_now - recalled)[:, None, :]
        output = jnp.einsum('hde,hd->he', state, query_now, precision=highest)
        return (state, output)
    initial = jnp.zeros((HEADS, HEAD_DIM, HEAD_DIM), jnp.float32)
    _, outputs = lax.scan(advance, initial, (query_rows, key_rows, value_rows, write_rates.astype(jnp.float32), is_start), unroll=8)
    outputs = outputs.reshape(SEQ_SLOTS, WIDTH)
    scale = lax.rsqrt(lax.optimization_barrier(jnp.mean(outputs * outputs, axis=1, keepdims=True)) + 1e-06)
    return (outputs * scale * norm_gain[None, :]).astype(jnp.bfloat16)
```

```python
import functools

import jax
import jax.numpy as jnp
from jax import lax
from jax.experimental import pallas as pl
from jax.experimental.pallas import tpu as pltpu
from jax.sharding import PartitionSpec as P

MESH = pl.DeviceIdType.MESH
F32, BF16 = jnp.float32, jnp.bfloat16
EPS = 1e-6
B = 128
NB = 8
ROWS = 8
WIDTH = 2048


def dotf(a, b):
    return lax.dot_general(a, b, (((1,), (0,)), ((), ())), preferred_element_type=F32)


def dot_nt(a, b):
    return lax.dot_general(a, b, (((1,), (1,)), ((), ())), preferred_element_type=F32)


def dot_tn(a, b):
    return lax.dot_general(a, b, (((0,), (0,)), ((), ())), preferred_element_type=F32)


def split(x):
    hi = x.astype(BF16)
    return hi, (x - hi.astype(F32)).astype(BF16)


def dot3(a, b):
    (ah, al), (bh, bl) = a, b
    return dotf(jnp.concatenate([ah, al], 1), jnp.concatenate([bh, bh], 0)) + dotf(ah, bl)


def combine(later, earlier):
    out = dot3(split(later[:, :B]), split(earlier))
    return jnp.concatenate([out[:, :B], out[:, B:] + later[:, B:]], 1)


def iota(shape, dim):
    return lax.broadcasted_iota(jnp.int32, shape, dim)


def invert(lows):
    row, col = iota((B, B), 0), iota((B, B), 1)
    near = (row // 8) == (col // 8)
    n = len(lows)
    parts = []
    for low in lows:
        c = jnp.sum(jnp.where(near, low, 0.0).reshape(16, 8, B), axis=0)
        hi = c.astype(BF16).astype(F32)
        parts += [hi, c - hi]
    stacked = jnp.concatenate(parts, 0).astype(BF16)
    spread = []
    for m in range(7):
        pick = jnp.where(near & (row % 8 == m), 1.0, 0.0).astype(BF16)
        spread.append(dotf(stacked, pick))
    eye8 = (iota((8, B), 1) % 8 == iota((8, B), 0)).astype(F32)
    inv = []
    for s in range(n):
        t = eye8
        for m in range(7):
            coef = spread[m][16 * s : 16 * s + 8] + spread[m][16 * s + 8 : 16 * s + 16]
            t = t - coef * t[m : m + 1]
        inv.append(jnp.where(near, jnp.concatenate([t] * 16, 0), 0.0))
    lsp = [split(low) for low in lows]
    for size in (8, 16, 32, 64):
        r, c = iota((64, B), 0), iota((64, B), 1)
        keep = (c // size) == 2 * (r // size)
        for s in range(n):
            t4 = inv[s].reshape(64 // size, 2, size, B)
            even, odd = t4[:, 0], t4[:, 1].reshape(64, B)
            x = jnp.where(keep, dot3(split(odd), lsp[s]), 0.0)
            odd = odd - dot3(split(x), split(inv[s]))
            inv[s] = jnp.concatenate(
                [even[:, None], odd.reshape(64 // size, 1, size, B)], 1
            ).reshape(B, B)
    return inv


def kernel(
    doc_ref, q_ref, k_ref, v_ref, rate_ref, gain_ref, o_ref,
    start_ref, wu_ref, map_ref, pre_ref, mat_ref, got_ref, ybuf_ref, ysend_ref, pz_ref,
    sout_ref, sbuf_ref, qp_ref, o1_ref, xsend_ref, xbuf_ref,
    g_send, g_recv, y_send, y_recv, s_send, s_recv, x_send, x_recv,
):
    ctx, head = lax.axis_index("ctx"), lax.axis_index("head")
    y, z = ctx // ROWS, lax.rem(ctx, ROWS)
    core = lax.rem(head, 2)

    def at_z(other):
        return {"ctx": y * ROWS + other}

    def at_y(other):
        return {"ctx": lax.rem(other, 4) * ROWS + z}

    def owner_z(h):
        return 4 * core + 2 * h

    mine = (z // 4 == core) & (lax.rem(z, 2) == 0)
    my_h = lax.rem(z, 4) // 2

    barrier = pltpu.get_barrier_semaphore()
    for i in range(1, ROWS):
        pl.semaphore_signal(barrier, 1, device_id=at_z(lax.rem(z + i, ROWS)), device_id_type=MESH)
    for i in range(1, 4):
        pl.semaphore_signal(barrier, 1, device_id=at_y(y + i), device_id_type=MESH)
    for i in range(1, 8):
        pl.semaphore_signal(barrier, 1, device_id={"head": lax.rem(head + i, 8)}, device_id_type=MESH)

    base = ctx * (NB * B)
    pos = base + iota((NB, B), 0) * B + iota((NB, B), 1)
    begin = jnp.int32(0)
    start = jnp.zeros((NB, B), jnp.int32)
    for m in range(31):
        begin = begin + doc_ref[m]
        start = jnp.where(pos >= begin, begin, start)
    start_f = (start - base).astype(F32)
    start_ref[...] = jnp.concatenate([start_f] * 16, 0).T

    row, col = iota((B, B), 0), iota((B, B), 1)
    row1 = iota((B, 1), 0).astype(F32)
    colf = col.astype(F32)

    def doc_columns(b):
        first = start_ref[:, b : b + 1]
        carry = (first < float(b * B)).astype(F32)
        last = (row1 + float(b * B) >= first[B - 1 : B]).astype(F32)
        return first, carry, last

    def lanes(h):
        return pl.ds(pl.multiple_of(h * B, B), B)

    def rate(b, h):
        r = rate_ref[pl.ds(b * B, B), :]
        return jnp.where(h == 0, r[:, 0:1], r[:, 1:2])

    def own_map(h):
        lows, rights = [], []
        for b in range(NB):
            kb = k_ref[pl.ds(b * B, B), lanes(h)]
            kf = kb.astype(F32)
            vf = v_ref[pl.ds(b * B, B), lanes(h)].astype(F32)
            rk = lax.rsqrt(jnp.sum(kf * kf, axis=1, keepdims=True) + EPS)
            beta = rate(b, h)
            first, _, _ = doc_columns(b)
            keep = (row > col) & (colf + float(b * B) >= first)
            scale = beta * rk
            lows.append(jnp.where(keep, dot_nt(kb, kb) * (scale * rk), 0.0))
            rights.append(split(jnp.concatenate([kf * (scale * rk), vf * scale], 1)))
        inv = invert(lows)
        maps = []
        for b in range(NB):
            wu = dot3(split(inv[b]), rights[b])
            _, carry, last = doc_columns(b)
            w, u = wu[:, :B] * carry, wu[:, B:]
            wu_ref[h, b] = jnp.concatenate([w, u], 1)
            hi, lo = split(jnp.concatenate([w * last, u * last], 1))
            kb = k_ref[pl.ds(b * B, B), lanes(h)]
            ma = dot_tn(jnp.concatenate([kb, kb], 0), jnp.concatenate([hi, lo], 0))
            m = jnp.where(row == col, carry[B - 1 : B], 0.0) - ma[:, :B]
            maps.append(jnp.concatenate([m, ma[:, B:]], 1))
            map_ref[h, b] = maps[b]
        pairs = [combine(maps[i + 1], maps[i]) for i in range(0, NB, 2)]
        p03 = combine(pairs[1], pairs[0])
        p47 = combine(pairs[3], pairs[2])
        total = combine(p47, p03)
        mat_ref[h, 0] = total[:, :B]
        mat_ref[h, 1] = total[:, B:]
        pre_ref[h, 1] = pairs[0]
        pre_ref[h, 3] = p03
        pre_ref[h, 4] = pairs[2]


    def send_map(h, part):
        return pltpu.make_async_remote_copy(
            src_ref=mat_ref.at[h, part], dst_ref=got_ref.at[z, part],
            send_sem=g_send.at[h, part], recv_sem=g_recv.at[z, part],
            device_id=at_z(owner_z(h)), device_id_type=MESH,
        )

    for h in range(2):
        own_map(h)
        if h == 0:
            pl.semaphore_wait(barrier, 17)

        @pl.when(z != owner_z(h))
        def _():
            send_map(h, 0).start()
            send_map(h, 1).start()

        @pl.when(z == owner_z(h))
        def _():
            got_ref[z] = mat_ref[h]

    def shadow(h):
        pre = [None, map_ref[h, 0], pre_ref[h, 1], None, pre_ref[h, 3], None, None, None]
        pre[3] = combine(map_ref[h, 2], pre[2])
        pre[5] = combine(map_ref[h, 4], pre[4])
        pre[6] = combine(pre_ref[h, 4], pre[4])
        pre[7] = combine(map_ref[h, 6], pre[6])
        for b in range(NB):
            kb = k_ref[pl.ds(b * B, B), lanes(h)]
            qb = q_ref[pl.ds(b * B, B), lanes(h)]
            qf = qb.astype(F32)
            rq = lax.rsqrt(jnp.sum(qf * qf, axis=1, keepdims=True) + EPS)
            first, carry, _ = doc_columns(b)
            keep = (row >= col) & (colf + float(b * B) >= first)
            sc = jnp.where(keep, dot_nt(qb, kb) * rq, 0.0)
            swu = dot3(split(sc), split(wu_ref[h, b]))
            qe = qf * (rq * carry) - swu[:, :B]
            o1 = swu[:, B:]
            if b > 0:
                qx = dot3(split(qe), split(pre[b]))
                qe = qx[:, :B]
                o1 = o1 + qx[:, B:]
            hi, lo = split(qe)
            qp_ref[h, pl.ds(b * B, B)] = jnp.concatenate([hi, lo], 1)
            o1_ref[h, pl.ds(b * B, B)] = o1

    for h in range(2):
        shadow(h)

    def send_y(src, slot, step):
        return pltpu.make_async_remote_copy(
            src_ref=ysend_ref.at[src], dst_ref=ybuf_ref.at[slot],
            send_sem=y_send.at[slot], recv_sem=y_recv.at[slot],
            device_id=at_y(y + step), device_id_type=MESH,
        )

    def send_state(i):
        to = lax.rem(z + i, ROWS)
        return pltpu.make_async_remote_copy(
            src_ref=sout_ref.at[to], dst_ref=sbuf_ref.at[my_h],
            send_sem=s_send.at[to], recv_sem=s_recv.at[my_h],
            device_id=at_z(to), device_id_type=MESH,
        )

    @pl.when(mine)
    def _():
        for i in range(1, ROWS):
            frm = lax.rem(z + i, ROWS)
            for part in range(2):
                pltpu.make_async_remote_copy(
                    src_ref=mat_ref.at[0, part], dst_ref=got_ref.at[frm, part],
                    send_sem=g_send.at[0, part], recv_sem=g_recv.at[frm, part],
                    device_id=at_z(frm), device_id_type=MESH,
                ).wait_recv()
        maps = [jnp.concatenate([got_ref[i, 0], got_ref[i, 1]], 1) for i in range(ROWS)]
        pairs = [combine(maps[i + 1], maps[i]) for i in range(0, ROWS, 2)]
        p03 = combine(pairs[1], pairs[0])
        p47 = combine(pairs[3], pairs[2])
        total = combine(p47, p03)
        ysend_ref[0] = total[:, :B]
        ysend_ref[1] = total[:, B:]
        sends = [send_y(0, 0, 1), send_y(1, 1, 1), send_y(1, 2, 2)]
        for c in sends:
            c.start()
        pre = [None, maps[0], pairs[0], None, p03, None, None, None]
        pre[3] = combine(maps[2], pre[2])
        pre[5] = combine(maps[4], pre[4])
        pre[6] = combine(pairs[2], pre[4])
        pre[7] = combine(maps[6], pre[6])
        for i in range(1, ROWS):
            pz_ref[i] = pre[i]
        for c in sends:
            c.wait()
        s_row = ybuf_ref[1] + dot3(split(ybuf_ref[0]), split(ybuf_ref[2]))
        sout_ref[0] = s_row
        s_split = split(s_row)
        for i in range(1, ROWS):
            p = pz_ref[i]
            sout_ref[i] = p[:, B:] + dot3(split(p[:, :B]), s_split)
        for i in range(1, ROWS):
            send_state(i).start()
        sbuf_ref[my_h] = sout_ref[z]

    for h in range(2):

        @pl.when(z != owner_z(h))
        def _():
            pltpu.make_async_remote_copy(
                src_ref=sout_ref.at[0], dst_ref=sbuf_ref.at[h],
                send_sem=s_send.at[0], recv_sem=s_recv.at[h],
                device_id=at_z(owner_z(h)), device_id_type=MESH,
            ).wait_recv()

    squares = [None] * NB
    for h in range(2):
        sh, sl = split(sbuf_ref[h])
        shh = jnp.concatenate([sh, sh], 0)
        for b in range(NB):
            rows = pl.ds(b * B, B)
            qp = qp_ref[h, rows]
            o = o1_ref[h, rows] + dotf(qp, shh) + dotf(qp[:, :B], sl)
            o1_ref[h, rows] = o
            squares[b] = o * o if h == 0 else squares[b] + o * o
    ones = jnp.ones((8, B), BF16)
    sub = iota((8, B), 0)
    sums = jnp.zeros((8, B), F32)
    for b in range(NB):
        hi, lo = split(squares[b])
        sums = jnp.where(sub == b, dot_nt(ones, hi) + dot_nt(ones, lo), sums)
    xsend_ref[...] = sums

    def send_x(i):
        return pltpu.make_async_remote_copy(
            src_ref=xsend_ref, dst_ref=xbuf_ref.at[i - 1],
            send_sem=x_send.at[i - 1], recv_sem=x_recv.at[i - 1],
            device_id={"head": lax.rem(head + i, 8)}, device_id_type=MESH,
        )

    for i in range(1, 8):
        send_x(i).start()
    for i in range(1, 8):
        send_x(i).wait()
        sums = sums + xbuf_ref[i - 1]
    scale = lax.rsqrt(sums / WIDTH + EPS)
    start_ref[...] = jnp.concatenate([scale] * 16, 0).T
    for h in range(2):
        gain = gain_ref[:, h * B : h * B + B]
        for b in range(NB):
            rows = pl.ds(b * B, B)
            o_ref[rows, h * B : h * B + B] = (
                o1_ref[h, rows] * start_ref[:, b : b + 1] * gain
            ).astype(BF16)

    for h in range(2):

        @pl.when(z != owner_z(h))
        def _():
            send_map(h, 0).wait_send()
            send_map(h, 1).wait_send()

    @pl.when(mine)
    def _():
        for i in range(1, ROWS):
            send_state(i).wait_send()


def local(queries, key_vectors, value_vectors, write_rates, doc_lengths, norm_gain):
    vm = pl.BlockSpec(memory_space=pltpu.VMEM)
    return pl.pallas_call(
        kernel,
        out_shape=jax.ShapeDtypeStruct(queries.shape, BF16),
        in_specs=[pl.BlockSpec(memory_space=pltpu.SMEM)] + [vm] * 5,
        out_specs=vm,
        scratch_shapes=[
            pltpu.VMEM((B, B), F32),
            pltpu.VMEM((2, NB, B, 2 * B), F32),
            pltpu.VMEM((2, NB, B, 2 * B), F32),
            pltpu.VMEM((2, 5, B, 2 * B), F32),
            pltpu.VMEM((2, 2, B, B), F32),
            pltpu.VMEM((ROWS, 2, B, B), F32),
            pltpu.VMEM((3, B, B), F32),
            pltpu.VMEM((2, B, B), F32),
            pltpu.VMEM((ROWS, B, 2 * B), F32),
            pltpu.VMEM((ROWS, B, B), F32),
            pltpu.VMEM((2, B, B), F32),
            pltpu.VMEM((2, NB * B, 2 * B), BF16),
            pltpu.VMEM((2, NB * B, B), F32),
            pltpu.VMEM((8, B), F32),
            pltpu.VMEM((7, 8, B), F32),
            pltpu.SemaphoreType.DMA((2, 2)),
            pltpu.SemaphoreType.DMA((ROWS, 2)),
            pltpu.SemaphoreType.DMA((3,)),
            pltpu.SemaphoreType.DMA((3,)),
            pltpu.SemaphoreType.DMA((ROWS,)),
            pltpu.SemaphoreType.DMA((2,)),
            pltpu.SemaphoreType.DMA((7,)),
            pltpu.SemaphoreType.DMA((7,)),
        ],
        compiler_params=pltpu.CompilerParams(
            collective_id=0, has_side_effects=True, vmem_limit_bytes=48 << 20
        ),
    )(doc_lengths, queries, key_vectors, value_vectors, write_rates, norm_gain[None])


def solution(mesh):
    tokens = P("ctx", "head")
    return jax.shard_map(
        local, mesh=mesh, in_specs=(tokens,) * 4 + (P(), P("head")), out_specs=tokens,
        check_vma=False,
    )
```

```python
import functools

import jax
import jax.numpy as jnp
from jax import lax
from jax.experimental import pallas as pl
from jax.experimental.pallas import tpu as pltpu
from jax.sharding import PartitionSpec as P

MESH = pl.DeviceIdType.MESH
F32, BF16 = jnp.float32, jnp.bfloat16
EPS = 1e-6
B = 128
NB = 8
ROWS = 8
WIDTH = 2048


def dotf(a, b):
    return lax.dot_general(a, b, (((1,), (0,)), ((), ())), preferred_element_type=F32)


def dot_nt(a, b):
    return lax.dot_general(a, b, (((1,), (1,)), ((), ())), preferred_element_type=F32)


def dot_tn(a, b):
    return lax.dot_general(a, b, (((0,), (0,)), ((), ())), preferred_element_type=F32)


def split(x):
    hi = x.astype(BF16)
    return hi, (x - hi.astype(F32)).astype(BF16)


def dot3(a, b):
    (ah, al), (bh, bl) = a, b
    return dotf(jnp.concatenate([ah, al], 1), jnp.concatenate([bh, bh], 0)) + dotf(ah, bl)


def combine(later, earlier):
    out = dot3(split(later[:, :B]), split(earlier))
    return jnp.concatenate([out[:, :B], out[:, B:] + later[:, B:]], 1)


def iota(shape, dim):
    return lax.broadcasted_iota(jnp.int32, shape, dim)


SIZES = (8, 16, 32, 64)


def stack_parts(x):
    hi = x.astype(BF16).astype(F32)
    return jnp.concatenate([hi, x - hi], 0).astype(BF16)


def dot_stacked(a, b):
    m, n = a.shape[0] // 2, b.shape[1] // 2
    r = dotf(a, b)
    return r[:m, :n] + (r[m:, :n] + r[:m, n:])


def invert(lows):
    row, col = iota((B, B), 0), iota((B, B), 1)
    n = len(lows)
    near = (row // 8) == (col // 8)
    parts = [
        stack_parts(jnp.sum(jnp.where(near, low, 0.0).reshape(16, 8, B), axis=0)) for low in lows
    ]
    lsp = [jnp.concatenate(split(low), 1) for low in lows]
    stacked = jnp.concatenate(parts, 0)
    spread = []
    for m in range(7):
        pick = jnp.where(near & (row % 8 == m), 1.0, 0.0).astype(BF16)
        r = dotf(stacked, pick).reshape(n, 2, 8, B)
        spread.append(r[:, 0] + r[:, 1])
    inv = jnp.broadcast_to((iota((8, B), 1) % 8 == iota((8, B), 0)).astype(F32), (n, 8, B))
    for m in range(7):
        inv = inv - spread[m] * inv[:, m : m + 1]
    inv = [inv[s] for s in range(n)]
    row2, col2 = iota((B, 2 * B), 0), iota((B, 2 * B), 1) % B
    for size in SIZES:
        below = (row2 // size == col2 // size + 1) & (row2 // size % 2 == 1)
        same = row2 // size == col2 // size
        odd = iota((size, B), 1) // size % 2 == 1
        xs, tops = [], []
        for s in range(n):
            upper = jnp.where(odd, 0.0, inv[s])
            inv[s] = jnp.where(odd, inv[s], 0.0)
            tops.append(upper)
            low = jnp.where(below, lsp[s], jnp.zeros_like(lsp[s]))
            xs.append(dot_stacked(stack_parts(inv[s]), low))
        for s in range(n):
            two = [tops[s]] * (16 // size if size < 16 else 1)
            two = jnp.concatenate(two, 0) if len(two) > 1 else two[0]
            wide = jnp.concatenate(split(two), 1)
            wide = jnp.concatenate([wide] * (B // wide.shape[0]), 0)
            wide = jnp.where(same, wide, jnp.zeros_like(wide))
            y = dot_stacked(stack_parts(xs[s]), wide)
            inv[s] = jnp.concatenate([tops[s], inv[s] - y], 0)
    return inv


def kernel(
    doc_ref, q_ref, k_ref, v_ref, rate_ref, gain_ref, o_ref,
    start_ref, wu_ref, map_ref, pre_ref, mat_ref, got_ref, ybuf_ref, ysend_ref, pz_ref,
    sout_ref, sbuf_ref, qp_ref, o1_ref, xsend_ref, xbuf_ref,
    g_send, g_recv, y_send, y_recv, s_send, s_recv, x_send, x_recv,
):
    ctx, head = lax.axis_index("ctx"), lax.axis_index("head")
    y, z = ctx // ROWS, lax.rem(ctx, ROWS)
    core = lax.rem(head, 2)

    def at_z(other):
        return {"ctx": y * ROWS + other}

    def at_y(other):
        return {"ctx": lax.rem(other, 4) * ROWS + z}

    def owner_z(h):
        return 4 * core + 2 * h

    mine = (z // 4 == core) & (lax.rem(z, 2) == 0)
    my_h = lax.rem(z, 4) // 2

    barrier = pltpu.get_barrier_semaphore()
    for i in range(1, ROWS):
        pl.semaphore_signal(barrier, 1, device_id=at_z(lax.rem(z + i, ROWS)), device_id_type=MESH)
    for i in range(1, 4):
        pl.semaphore_signal(barrier, 1, device_id=at_y(y + i), device_id_type=MESH)
    for i in range(1, 8):
        pl.semaphore_signal(barrier, 1, device_id={"head": lax.rem(head + i, 8)}, device_id_type=MESH)

    base = ctx * (NB * B)
    pos = base + iota((NB, B), 0) * B + iota((NB, B), 1)
    begin = jnp.int32(0)
    start = jnp.zeros((NB, B), jnp.int32)
    for m in range(31):
        begin = begin + doc_ref[m]
        start = jnp.where(pos >= begin, begin, start)
    start_f = (start - base).astype(F32)
    start_ref[...] = jnp.concatenate([start_f] * 16, 0).T

    row, col = iota((B, B), 0), iota((B, B), 1)
    row1 = iota((B, 1), 0).astype(F32)
    colf = col.astype(F32)

    def doc_columns(b):
        first = start_ref[:, b : b + 1]
        carry = (first < float(b * B)).astype(F32)
        last = (row1 + float(b * B) >= first[B - 1 : B]).astype(F32)
        return first, carry, last

    def lanes(h):
        return pl.ds(pl.multiple_of(h * B, B), B)

    def rate(b, h):
        r = rate_ref[pl.ds(b * B, B), :]
        return jnp.where(h == 0, r[:, 0:1], r[:, 1:2])

    def own_map(h):
        lows, rights = [], []
        for b in range(NB):
            kb = k_ref[pl.ds(b * B, B), lanes(h)]
            kf = kb.astype(F32)
            vf = v_ref[pl.ds(b * B, B), lanes(h)].astype(F32)
            rk = lax.rsqrt(jnp.sum(kf * kf, axis=1, keepdims=True) + EPS)
            beta = rate(b, h)
            first, _, _ = doc_columns(b)
            keep = (row > col) & (colf + float(b * B) >= first)
            scale = beta * rk
            lows.append(jnp.where(keep, dot_nt(kb, kb) * (scale * rk), 0.0))
            rights.append(split(jnp.concatenate([kf * (scale * rk), vf * scale], 1)))
        inv = invert(lows)
        maps, wus = [], []
        for b in range(NB):
            wus.append(dot3(split(inv[b]), rights[b]))
        for b in range(NB):
            _, carry, last = doc_columns(b)
            w, u = wus[b][:, :B] * carry, wus[b][:, B:]
            wu_ref[h, b] = jnp.concatenate([w, u], 1)
            hi, lo = split(jnp.concatenate([w * last, u * last], 1))
            kt = k_ref[pl.ds(b * B, B), lanes(h)].T
            ma = dotf(jnp.concatenate([kt, kt], 1), jnp.concatenate([hi, lo], 0))
            m = jnp.where(row == col, carry[B - 1 : B], 0.0) - ma[:, :B]
            maps.append(jnp.concatenate([m, ma[:, B:]], 1))
            map_ref[h, b] = maps[b]
        pairs = [combine(maps[i + 1], maps[i]) for i in range(0, NB, 2)]
        p03 = combine(pairs[1], pairs[0])
        p47 = combine(pairs[3], pairs[2])
        total = combine(p47, p03)
        mat_ref[h, 0] = total[:, :B]
        mat_ref[h, 1] = total[:, B:]
        pre_ref[h, 1] = pairs[0]
        pre_ref[h, 3] = p03
        pre_ref[h, 4] = pairs[2]


    def send_map(h, part):
        return pltpu.make_async_remote_copy(
            src_ref=mat_ref.at[h, part], dst_ref=got_ref.at[z, part],
            send_sem=g_send.at[h, part], recv_sem=g_recv.at[z, part],
            device_id=at_z(owner_z(h)), device_id_type=MESH,
        )

    for h in range(2):
        own_map(h)
        if h == 0:
            pl.semaphore_wait(barrier, 17)

        @pl.when(z != owner_z(h))
        def _():
            send_map(h, 0).start()
            send_map(h, 1).start()

        @pl.when(z == owner_z(h))
        def _():
            got_ref[z] = mat_ref[h]

    def shadow(h):
        pre = [None, map_ref[h, 0], pre_ref[h, 1], None, pre_ref[h, 3], None, None, None]
        pre[3] = combine(map_ref[h, 2], pre[2])
        pre[5] = combine(map_ref[h, 4], pre[4])
        pre[6] = combine(pre_ref[h, 4], pre[4])
        scores, lefts = [], []
        for b in range(NB):
            kb = k_ref[pl.ds(b * B, B), lanes(h)]
            qb = q_ref[pl.ds(b * B, B), lanes(h)]
            qf = qb.astype(F32)
            rq = lax.rsqrt(jnp.sum(qf * qf, axis=1, keepdims=True) + EPS)
            first, carry, _ = doc_columns(b)
            keep = (row >= col) & (colf + float(b * B) >= first)
            scores.append(jnp.where(keep, dot_nt(qb, kb) * rq, 0.0))
            lefts.append(qf * (rq * carry))
        pre[7] = combine(map_ref[h, 6], pre[6])
        both = [dot3(split(scores[b]), split(wu_ref[h, b])) for b in range(NB)]
        qes = [lefts[b] - both[b][:, :B] for b in range(NB)]
        o1s = [both[b][:, B:] for b in range(NB)]
        qxs = [dot3(split(qes[b]), split(pre[b])) for b in range(1, NB)]
        for b in range(NB):
            qe, o1 = qes[b], o1s[b]
            if b > 0:
                qe, o1 = qxs[b - 1][:, :B], o1 + qxs[b - 1][:, B:]
            hi, lo = split(qe)
            qp_ref[h, pl.ds(b * B, B)] = jnp.concatenate([hi, lo], 1)
            o1_ref[h, pl.ds(b * B, B)] = o1

    for h in range(2):
        shadow(h)

    def send_y(src, slot, step):
        return pltpu.make_async_remote_copy(
            src_ref=ysend_ref.at[src], dst_ref=ybuf_ref.at[slot],
            send_sem=y_send.at[slot], recv_sem=y_recv.at[slot],
            device_id=at_y(y + step), device_id_type=MESH,
        )

    def send_state(i):
        to = lax.rem(z + i, ROWS)
        return pltpu.make_async_remote_copy(
            src_ref=sout_ref.at[to], dst_ref=sbuf_ref.at[my_h],
            send_sem=s_send.at[to], recv_sem=s_recv.at[my_h],
            device_id=at_z(to), device_id_type=MESH,
        )

    @pl.when(mine)
    def _():
        for i in range(1, ROWS):
            frm = lax.rem(z + i, ROWS)
            for part in range(2):
                pltpu.make_async_remote_copy(
                    src_ref=mat_ref.at[0, part], dst_ref=got_ref.at[frm, part],
                    send_sem=g_send.at[0, part], recv_sem=g_recv.at[frm, part],
                    device_id=at_z(frm), device_id_type=MESH,
                ).wait_recv()
        maps = [jnp.concatenate([got_ref[i, 0], got_ref[i, 1]], 1) for i in range(ROWS)]
        pairs = [combine(maps[i + 1], maps[i]) for i in range(0, ROWS, 2)]
        p03 = combine(pairs[1], pairs[0])
        p47 = combine(pairs[3], pairs[2])
        total = combine(p47, p03)
        ysend_ref[0] = total[:, :B]
        ysend_ref[1] = total[:, B:]
        sends = [send_y(0, 0, 1), send_y(1, 1, 1), send_y(1, 2, 2)]
        for c in sends:
            c.start()
        pre = [None, maps[0], pairs[0], None, p03, None, None, None]
        pre[3] = combine(maps[2], pre[2])
        pre[5] = combine(maps[4], pre[4])
        pre[6] = combine(pairs[2], pre[4])
        pre[7] = combine(maps[6], pre[6])
        for i in range(1, ROWS):
            pz_ref[i] = pre[i]
        for c in sends:
            c.wait()
        s_row = ybuf_ref[1] + dot3(split(ybuf_ref[0]), split(ybuf_ref[2]))
        sout_ref[0] = s_row
        s_split = split(s_row)
        for i in range(1, ROWS):
            p = pz_ref[i]
            sout_ref[i] = p[:, B:] + dot3(split(p[:, :B]), s_split)
        for i in range(1, ROWS):
            send_state(i).start()
        sbuf_ref[my_h] = sout_ref[z]

    for h in range(2):

        @pl.when(z != owner_z(h))
        def _():
            pltpu.make_async_remote_copy(
                src_ref=sout_ref.at[0], dst_ref=sbuf_ref.at[h],
                send_sem=s_send.at[0], recv_sem=s_recv.at[h],
                device_id=at_z(owner_z(h)), device_id_type=MESH,
            ).wait_recv()

    squares = [None] * NB
    for h in range(2):
        sh, sl = split(sbuf_ref[h])
        shh = jnp.concatenate([sh, sh], 0)
        for b in range(NB):
            rows = pl.ds(b * B, B)
            qp = qp_ref[h, rows]
            o = o1_ref[h, rows] + dotf(qp, shh) + dotf(qp[:, :B], sl)
            o1_ref[h, rows] = o
            squares[b] = o * o if h == 0 else squares[b] + o * o
    ones = jnp.ones((8, B), BF16)
    sub = iota((8, B), 0)
    sums = jnp.zeros((8, B), F32)
    for b in range(NB):
        hi, lo = split(squares[b])
        sums = jnp.where(sub == b, dot_nt(ones, hi) + dot_nt(ones, lo), sums)
    xsend_ref[...] = sums

    def send_x(i):
        return pltpu.make_async_remote_copy(
            src_ref=xsend_ref, dst_ref=xbuf_ref.at[i - 1],
            send_sem=x_send.at[i - 1], recv_sem=x_recv.at[i - 1],
            device_id={"head": lax.rem(head + i, 8)}, device_id_type=MESH,
        )

    for i in range(1, 8):
        send_x(i).start()
    for i in range(1, 8):
        send_x(i).wait()
        sums = sums + xbuf_ref[i - 1]
    scale = lax.rsqrt(sums / WIDTH + EPS)
    start_ref[...] = jnp.concatenate([scale] * 16, 0).T
    for h in range(2):
        gain = gain_ref[:, h * B : h * B + B]
        for b in range(NB):
            rows = pl.ds(b * B, B)
            o_ref[rows, h * B : h * B + B] = (
                o1_ref[h, rows] * start_ref[:, b : b + 1] * gain
            ).astype(BF16)

    for h in range(2):

        @pl.when(z != owner_z(h))
        def _():
            send_map(h, 0).wait_send()
            send_map(h, 1).wait_send()

    @pl.when(mine)
    def _():
        for i in range(1, ROWS):
            send_state(i).wait_send()


def local(queries, key_vectors, value_vectors, write_rates, doc_lengths, norm_gain):
    vm = pl.BlockSpec(memory_space=pltpu.VMEM)
    return pl.pallas_call(
        kernel,
        out_shape=jax.ShapeDtypeStruct(queries.shape, BF16),
        in_specs=[pl.BlockSpec(memory_space=pltpu.SMEM)] + [vm] * 5,
        out_specs=vm,
        scratch_shapes=[
            pltpu.VMEM((B, B), F32),
            pltpu.VMEM((2, NB, B, 2 * B), F32),
            pltpu.VMEM((2, NB, B, 2 * B), F32),
            pltpu.VMEM((2, 5, B, 2 * B), F32),
            pltpu.VMEM((2, 2, B, B), F32),
            pltpu.VMEM((ROWS, 2, B, B), F32),
            pltpu.VMEM((3, B, B), F32),
            pltpu.VMEM((2, B, B), F32),
            pltpu.VMEM((ROWS, B, 2 * B), F32),
            pltpu.VMEM((ROWS, B, B), F32),
            pltpu.VMEM((2, B, B), F32),
            pltpu.VMEM((2, NB * B, 2 * B), BF16),
            pltpu.VMEM((2, NB * B, B), F32),
            pltpu.VMEM((8, B), F32),
            pltpu.VMEM((7, 8, B), F32),
            pltpu.SemaphoreType.DMA((2, 2)),
            pltpu.SemaphoreType.DMA((ROWS, 2)),
            pltpu.SemaphoreType.DMA((3,)),
            pltpu.SemaphoreType.DMA((3,)),
            pltpu.SemaphoreType.DMA((ROWS,)),
            pltpu.SemaphoreType.DMA((2,)),
            pltpu.SemaphoreType.DMA((7,)),
            pltpu.SemaphoreType.DMA((7,)),
        ],
        compiler_params=pltpu.CompilerParams(
            collective_id=0, has_side_effects=True, vmem_limit_bytes=48 << 20
        ),
    )(doc_lengths, queries, key_vectors, value_vectors, write_rates, norm_gain[None])


def solution(mesh):
    tokens = P("ctx", "head")
    return jax.shard_map(
        local, mesh=mesh, in_specs=(tokens,) * 4 + (P(), P("head")), out_specs=tokens,
        check_vma=False,
    )
```

```python
import functools

import jax
import jax.numpy as jnp
from jax import lax
from jax.experimental import pallas as pl
from jax.experimental.pallas import tpu as pltpu
from jax.sharding import PartitionSpec as P

MESH = pl.DeviceIdType.MESH
F32, BF16 = jnp.float32, jnp.bfloat16
EPS = 1e-6
B = 128
NB = 8
ROWS = 8
WIDTH = 2048


def dotf(a, b):
    return lax.dot_general(a, b, (((1,), (0,)), ((), ())), preferred_element_type=F32)


def dot_nt(a, b):
    return lax.dot_general(a, b, (((1,), (1,)), ((), ())), preferred_element_type=F32)


def dot_tn(a, b):
    return lax.dot_general(a, b, (((0,), (0,)), ((), ())), preferred_element_type=F32)


def split(x):
    hi = x.astype(BF16)
    return hi, (x - hi.astype(F32)).astype(BF16)


def dot3(a, b):
    (ah, al), (bh, bl) = a, b
    return dotf(jnp.concatenate([ah, al], 1), jnp.concatenate([bh, bh], 0)) + dotf(ah, bl)


def combine(later, earlier):
    out = dot3(split(later[:, :B]), split(earlier))
    return jnp.concatenate([out[:, :B], out[:, B:] + later[:, B:]], 1)


def iota(shape, dim):
    return lax.broadcasted_iota(jnp.int32, shape, dim)


SIZES = (8, 16, 32, 64)


def stack_parts(x):
    hi = x.astype(BF16).astype(F32)
    return jnp.concatenate([hi, x - hi], 0).astype(BF16)


def dot_stacked(a, b):
    m, n = a.shape[0] // 2, b.shape[1] // 2
    r = dotf(a, b)
    return r[:m, :n] + (r[m:, :n] + r[:m, n:])


def invert(lows):
    row, col = iota((B, B), 0), iota((B, B), 1)
    n = len(lows)
    near = (row // 8) == (col // 8)
    parts = [
        stack_parts(jnp.sum(jnp.where(near, low, 0.0).reshape(16, 8, B), axis=0)) for low in lows
    ]
    lsp = [jnp.concatenate(split(low), 1) for low in lows]
    stacked = jnp.concatenate(parts, 0)
    spread = []
    for m in range(7):
        pick = jnp.where(near & (row % 8 == m), 1.0, 0.0).astype(BF16)
        r = dotf(stacked, pick).reshape(n, 2, 8, B)
        spread.append(r[:, 0] + r[:, 1])
    inv = jnp.broadcast_to((iota((8, B), 1) % 8 == iota((8, B), 0)).astype(F32), (n, 8, B))
    for m in range(7):
        inv = inv - spread[m] * inv[:, m : m + 1]
    inv = [inv[s] for s in range(n)]
    row2, col2 = iota((B, 2 * B), 0), iota((B, 2 * B), 1) % B
    for size in SIZES:
        below = (row2 // size == col2 // size + 1) & (row2 // size % 2 == 1)
        same = row2 // size == col2 // size
        odd = iota((size, B), 1) // size % 2 == 1
        xs, tops = [], []
        for s in range(n):
            upper = jnp.where(odd, 0.0, inv[s])
            inv[s] = jnp.where(odd, inv[s], 0.0)
            tops.append(upper)
            low = jnp.where(below, lsp[s], jnp.zeros_like(lsp[s]))
            xs.append(dot_stacked(stack_parts(inv[s]), low))
        for s in range(n):
            two = [tops[s]] * (16 // size if size < 16 else 1)
            two = jnp.concatenate(two, 0) if len(two) > 1 else two[0]
            wide = jnp.concatenate(split(two), 1)
            wide = jnp.concatenate([wide] * (B // wide.shape[0]), 0)
            wide = jnp.where(same, wide, jnp.zeros_like(wide))
            y = dot_stacked(stack_parts(xs[s]), wide)
            inv[s] = jnp.concatenate([tops[s], inv[s] - y], 0)
    return inv


def kernel(
    doc_ref, q_hbm, k_hbm, v_hbm, rate_hbm, gain_hbm, o_ref,
    q_ref, k_ref, v_ref, rate_ref, gain_ref, cols_ref, scale_ref, wu_ref, map_ref, pre_ref, mat_ref, got_ref, ybuf_ref, ysend_ref, pm_ref, pa_ref,
    sout_ref, sbuf_ref, qp_ref, o1_ref, xsend_ref, xbuf_ref,
    in_sem, g_send, g_recv, y_send, y_recv, s_send, s_recv, x_send, x_recv,
):
    def load(i, hbm, ref, h):
        if h is not None:
            hbm, ref = hbm.at[:, h * B : h * B + B], ref.at[:, h * B : h * B + B]
        return pltpu.make_async_copy(hbm, ref, in_sem.at[i])

    loads = [
        load(0, rate_hbm, rate_ref, None),
        load(1, k_hbm, k_ref, 0),
        load(2, v_hbm, v_ref, 0),
        load(3, k_hbm, k_ref, 1),
        load(4, v_hbm, v_ref, 1),
        load(5, gain_hbm, gain_ref, None),
        load(6, q_hbm, q_ref, None),
    ]
    for copy in loads:
        copy.start()
    ctx, head = lax.axis_index("ctx"), lax.axis_index("head")
    y, z = ctx // ROWS, lax.rem(ctx, ROWS)
    core = lax.rem(head, 2)

    def at_z(other):
        return {"ctx": y * ROWS + other}

    def at_y(other):
        return {"ctx": lax.rem(other, 4) * ROWS + z}

    def owner_z(h):
        return 4 * core + 2 * h

    mine = (z // 4 == core) & (lax.rem(z, 2) == 0)
    my_h = lax.rem(z, 4) // 2

    barrier = pltpu.get_barrier_semaphore()
    for i in range(1, ROWS):
        pl.semaphore_signal(barrier, 1, device_id=at_z(lax.rem(z + i, ROWS)), device_id_type=MESH)
    for i in range(1, 4):
        pl.semaphore_signal(barrier, 1, device_id=at_y(y + i), device_id_type=MESH)
    for i in range(1, 8):
        pl.semaphore_signal(barrier, 1, device_id={"head": lax.rem(head + i, 8)}, device_id_type=MESH)

    base = ctx * (NB * B)
    pos = base + iota((NB, B), 0) * B + iota((NB, B), 1)
    begin = jnp.int32(0)
    start = jnp.zeros((NB, B), jnp.int32)
    for m in range(31):
        begin = begin + doc_ref[m]
        start = jnp.where(pos >= begin, begin, start)
    loads[0].wait()
    rates = [rate_ref[h : h + 1, b * B : b * B + B] for h in range(2) for b in range(NB)]
    start_f = (start - base).astype(F32)
    cols_ref[...] = jnp.concatenate([start_f] + rates + [start_f] * 13, 0).T

    row, col = iota((B, B), 0), iota((B, B), 1)
    eye = (row == col).astype(F32)
    row1 = iota((B, 1), 0).astype(F32)
    colf = col.astype(F32)

    def doc_columns(b):
        first = cols_ref[:, b : b + 1]
        carry = (first < float(b * B)).astype(F32)
        last = (row1 + float(b * B) >= first[B - 1 : B]).astype(F32)
        return first, carry, last

    def lanes(h):
        return pl.ds(pl.multiple_of(h * B, B), B)

    def rate(b, h):
        i = NB + h * NB + b
        return cols_ref[:, i : i + 1]

    def own_map(h):
        lows, rights = [], []
        for b in range(NB):
            kb = k_ref[pl.ds(b * B, B), lanes(h)]
            kf = kb.astype(F32)
            vf = v_ref[pl.ds(b * B, B), lanes(h)].astype(F32)
            rk = lax.rsqrt(jnp.sum(kf * kf, axis=1, keepdims=True) + EPS)
            beta = rate(b, h)
            first, _, _ = doc_columns(b)
            keep = (row > col) & (colf + float(b * B) >= first)
            scale = beta * rk
            lows.append(jnp.where(keep, dot_nt(kb, kb) * (scale * rk), 0.0))
            rights.append(split(jnp.concatenate([kf * (scale * rk), vf * scale], 1)))
        inv = invert(lows)
        maps, wus = [], []
        for b in range(NB):
            wus.append(dot3(split(inv[b]), rights[b]))
        for b in range(NB):
            _, carry, last = doc_columns(b)
            w, u = wus[b][:, :B] * carry, wus[b][:, B:]
            wu_ref[h, b] = jnp.concatenate([w, u], 1)
            hi, lo = split(jnp.concatenate([w * last, u * last], 1))
            kt = k_ref[pl.ds(b * B, B), lanes(h)].T
            ma = dotf(jnp.concatenate([kt, kt], 1), jnp.concatenate([hi, lo], 0))
            m = jnp.where(row == col, carry[B - 1 : B], 0.0) - ma[:, :B]
            maps.append(jnp.concatenate([m, ma[:, B:]], 1))
            map_ref[h, b] = maps[b]
        pairs = [combine(maps[i + 1], maps[i]) for i in range(0, NB, 2)]
        p03 = combine(pairs[1], pairs[0])
        p47 = combine(pairs[3], pairs[2])
        total = combine(p47, p03)
        mat_ref[h, 0] = total[:, :B]
        mat_ref[h, 1] = total[:, B:]
        pre_ref[h, 1] = pairs[0]
        pre_ref[h, 3] = p03
        pre_ref[h, 4] = pairs[2]


    def send_map(h, part):
        return pltpu.make_async_remote_copy(
            src_ref=mat_ref.at[h, part], dst_ref=got_ref.at[z, part],
            send_sem=g_send.at[h, part], recv_sem=g_recv.at[z, part],
            device_id=at_z(owner_z(h)), device_id_type=MESH,
        )

    for h in range(2):
        loads[1 + 2 * h].wait()
        loads[2 + 2 * h].wait()
        own_map(h)
        if h == 0:
            pl.semaphore_wait(barrier, 17)

        @pl.when(z != owner_z(h))
        def _():
            send_map(h, 0).start()
            send_map(h, 1).start()

        @pl.when(z == owner_z(h))
        def _():
            got_ref[z] = mat_ref[h]

    def shadow(h):
        pre = [None, map_ref[h, 0], pre_ref[h, 1], None, pre_ref[h, 3], None, None, None]
        pre[3] = combine(map_ref[h, 2], pre[2])
        pre[5] = combine(map_ref[h, 4], pre[4])
        pre[6] = combine(pre_ref[h, 4], pre[4])
        scores, lefts = [], []
        for b in range(NB):
            kb = k_ref[pl.ds(b * B, B), lanes(h)]
            qb = q_ref[pl.ds(b * B, B), lanes(h)]
            qf = qb.astype(F32)
            rq = lax.rsqrt(jnp.sum(qf * qf, axis=1, keepdims=True) + EPS)
            first, carry, _ = doc_columns(b)
            keep = (row >= col) & (colf + float(b * B) >= first)
            scores.append(jnp.where(keep, dot_nt(qb, kb) * rq, 0.0))
            lefts.append(qf * (rq * carry))
        pre[7] = combine(map_ref[h, 6], pre[6])
        both = [dot3(split(scores[b]), split(wu_ref[h, b])) for b in range(NB)]
        qes = [lefts[b] - both[b][:, :B] for b in range(NB)]
        o1s = [both[b][:, B:] for b in range(NB)]
        qxs = [dot3(split(qes[b]), split(pre[b])) for b in range(1, NB)]
        for b in range(NB):
            qe, o1 = qes[b], o1s[b]
            if b > 0:
                qe, o1 = qxs[b - 1][:, :B], o1 + qxs[b - 1][:, B:]
            hi, lo = split(qe)
            qp_ref[h, pl.ds(b * B, B)] = jnp.concatenate([hi, lo], 1)
            o1_ref[h, pl.ds(b * B, B)] = o1

    loads[5].wait()
    loads[6].wait()
    for h in range(2):
        shadow(h)

    def send_y(src, slot, step):
        return pltpu.make_async_remote_copy(
            src_ref=ysend_ref.at[src], dst_ref=ybuf_ref.at[slot],
            send_sem=y_send.at[slot], recv_sem=y_recv.at[slot],
            device_id=at_y(y + step), device_id_type=MESH,
        )

    def send_state(i):
        to = lax.rem(z + i, ROWS)
        return pltpu.make_async_remote_copy(
            src_ref=sout_ref.at[to], dst_ref=sbuf_ref.at[my_h],
            send_sem=s_send.at[to], recv_sem=s_recv.at[my_h],
            device_id=at_z(to), device_id_type=MESH,
        )

    @pl.when(mine)
    def _():
        for i in range(1, ROWS):
            frm = lax.rem(z + i, ROWS)
            for part in range(2):
                pltpu.make_async_remote_copy(
                    src_ref=mat_ref.at[0, part], dst_ref=got_ref.at[frm, part],
                    send_sem=g_send.at[0, part], recv_sem=g_recv.at[frm, part],
                    device_id=at_z(frm), device_id_type=MESH,
                ).wait_recv()
        maps = [jnp.concatenate([got_ref[i, 0], got_ref[i, 1]], 1) for i in range(ROWS)]
        pairs = [combine(maps[i + 1], maps[i]) for i in range(0, ROWS, 2)]
        p03 = combine(pairs[1], pairs[0])
        p47 = combine(pairs[3], pairs[2])
        total = combine(p47, p03)
        ysend_ref[0] = total[:, :B]
        ysend_ref[1] = total[:, B:]
        sends = [send_y(0, 0, 1), send_y(1, 1, 1), send_y(1, 2, 2)]
        for c in sends:
            c.start()
        pre = [None, maps[0], pairs[0], None, p03, None, None, None]
        pre[3] = combine(maps[2], pre[2])
        pre[5] = combine(maps[4], pre[4])
        pre[6] = combine(pairs[2], pre[4])
        pre[7] = combine(maps[6], pre[6])
        for i in range(ROWS):
            p = pre[i] if i else jnp.concatenate([eye, jnp.zeros_like(eye)], 1)
            pm_ref[i] = jnp.concatenate(split(p[:, :B]), 1)
            pa_ref[i] = p[:, B:]
        for c in sends:
            c.wait()
        s_row = ybuf_ref[1] + dot3(split(ybuf_ref[0]), split(ybuf_ref[2]))
        sh, sl = split(s_row)
        shh = jnp.concatenate([sh, sh], 0)
        for i in (4, 3, 5, 2, 6, 1, 7, 0):
            to = lax.rem(z + i, ROWS)
            pm = pm_ref[to]
            sout_ref[to] = pa_ref[to] + dotf(pm, shh) + dotf(pm[:, :B], sl)
            if i:
                send_state(i).start()
        sbuf_ref[my_h] = sout_ref[z]

    for h in range(2):

        @pl.when(z != owner_z(h))
        def _():
            pltpu.make_async_remote_copy(
                src_ref=sout_ref.at[0], dst_ref=sbuf_ref.at[h],
                send_sem=s_send.at[0], recv_sem=s_recv.at[h],
                device_id=at_z(owner_z(h)), device_id_type=MESH,
            ).wait_recv()

    squares = [None] * NB
    for h in range(2):
        sh, sl = split(sbuf_ref[h])
        shh = jnp.concatenate([sh, sh], 0)
        for b in range(NB):
            rows = pl.ds(b * B, B)
            qp = qp_ref[h, rows]
            o = o1_ref[h, rows] + dotf(qp, shh) + dotf(qp[:, :B], sl)
            o1_ref[h, rows] = o
            squares[b] = o * o if h == 0 else squares[b] + o * o
    ones = jnp.ones((8, B), BF16)
    sub = iota((8, B), 0)
    sums = jnp.zeros((8, B), F32)
    for b in range(NB):
        hi, lo = split(squares[b])
        sums = jnp.where(sub == b, dot_nt(ones, hi) + dot_nt(ones, lo), sums)
    xsend_ref[...] = sums

    def send_x(i):
        return pltpu.make_async_remote_copy(
            src_ref=xsend_ref, dst_ref=xbuf_ref.at[i - 1],
            send_sem=x_send.at[i - 1], recv_sem=x_recv.at[i - 1],
            device_id={"head": lax.rem(head + i, 8)}, device_id_type=MESH,
        )

    for i in range(1, 8):
        send_x(i).start()
    for i in range(1, 8):
        send_x(i).wait()
        sums = sums + xbuf_ref[i - 1]
    scale = lax.rsqrt(sums / WIDTH + EPS)
    scale_ref[...] = jnp.concatenate([scale] * 16, 0).T
    for h in range(2):
        gain = gain_ref[:, h * B : h * B + B]
        for b in range(NB):
            rows = pl.ds(b * B, B)
            o_ref[rows, h * B : h * B + B] = (
                o1_ref[h, rows] * scale_ref[:, b : b + 1] * gain
            ).astype(BF16)

    for h in range(2):

        @pl.when(z != owner_z(h))
        def _():
            send_map(h, 0).wait_send()
            send_map(h, 1).wait_send()

    @pl.when(mine)
    def _():
        for i in range(1, ROWS):
            send_state(i).wait_send()


def local(queries, key_vectors, value_vectors, write_rates, doc_lengths, norm_gain):
    vm = pl.BlockSpec(memory_space=pltpu.VMEM)
    return pl.pallas_call(
        kernel,
        out_shape=pltpu.VMEM(queries.shape, BF16),
        in_specs=[pl.BlockSpec(memory_space=pltpu.SMEM)]
        + [pl.BlockSpec(memory_space=pltpu.HBM)] * 5,
        out_specs=vm,
        scratch_shapes=[
            pltpu.VMEM((NB * B, 2 * B), BF16),
            pltpu.VMEM((NB * B, 2 * B), BF16),
            pltpu.VMEM((NB * B, 2 * B), BF16),
            pltpu.VMEM((2, NB * B), F32),
            pltpu.VMEM((1, 2 * B), F32),
            pltpu.VMEM((B, B), F32),
            pltpu.VMEM((B, B), F32),
            pltpu.VMEM((2, NB, B, 2 * B), F32),
            pltpu.VMEM((2, NB, B, 2 * B), F32),
            pltpu.VMEM((2, 5, B, 2 * B), F32),
            pltpu.VMEM((2, 2, B, B), F32),
            pltpu.VMEM((ROWS, 2, B, B), F32),
            pltpu.VMEM((3, B, B), F32),
            pltpu.VMEM((2, B, B), F32),
            pltpu.VMEM((ROWS, B, 2 * B), BF16),
            pltpu.VMEM((ROWS, B, B), F32),
            pltpu.VMEM((ROWS, B, B), F32),
            pltpu.VMEM((2, B, B), F32),
            pltpu.VMEM((2, NB * B, 2 * B), BF16),
            pltpu.VMEM((2, NB * B, B), F32),
            pltpu.VMEM((8, B), F32),
            pltpu.VMEM((7, 8, B), F32),
            pltpu.SemaphoreType.DMA((7,)),
            pltpu.SemaphoreType.DMA((2, 2)),
            pltpu.SemaphoreType.DMA((ROWS, 2)),
            pltpu.SemaphoreType.DMA((3,)),
            pltpu.SemaphoreType.DMA((3,)),
            pltpu.SemaphoreType.DMA((ROWS,)),
            pltpu.SemaphoreType.DMA((2,)),
            pltpu.SemaphoreType.DMA((7,)),
            pltpu.SemaphoreType.DMA((7,)),
        ],
        compiler_params=pltpu.CompilerParams(
            collective_id=0, has_side_effects=True, vmem_limit_bytes=63 << 20
        ),
    )(doc_lengths, queries, key_vectors, value_vectors, write_rates.T, norm_gain[None])


def solution(mesh):
    tokens = P("ctx", "head")
    return jax.shard_map(
        local, mesh=mesh, in_specs=(tokens,) * 4 + (P(), P("head")), out_specs=tokens,
        check_vma=False,
    )
```

```python
import functools

import jax
import jax.numpy as jnp
from jax import lax
from jax.experimental import pallas as pl
from jax.experimental.pallas import tpu as pltpu
from jax.sharding import PartitionSpec as P

MESH = pl.DeviceIdType.MESH
F32, BF16 = jnp.float32, jnp.bfloat16
EPS = 1e-6
B = 128
NB = 8
ROWS = 8
WIDTH = 2048


def dotf(a, b):
    return lax.dot_general(a, b, (((1,), (0,)), ((), ())), preferred_element_type=F32)


def dot_nt(a, b):
    return lax.dot_general(a, b, (((1,), (1,)), ((), ())), preferred_element_type=F32)


def dot_tn(a, b):
    return lax.dot_general(a, b, (((0,), (0,)), ((), ())), preferred_element_type=F32)


def split(x):
    hi = x.astype(BF16)
    return hi, (x - hi.astype(F32)).astype(BF16)


def dot3(a, b):
    (ah, al), (bh, bl) = a, b
    return dotf(jnp.concatenate([ah, al], 1), jnp.concatenate([bh, bh], 0)) + dotf(ah, bl)


def wide(x):
    return jnp.concatenate(split(x), 1)


def dotw(a, b):
    n = b.shape[1] // 2
    r = dotf(a, jnp.concatenate([b, b], 0))
    return r[:, :n] + r[:, n:]


def products(ms):
    w = [wide(m) for m in ms]
    m01, m23, m45, m67 = [dotw(w[i + 1], w[i]) for i in range(0, 8, 2)]
    w01, w23, w45, w67 = [wide(m) for m in (m01, m23, m45, m67)]
    m03, m47 = dotw(w23, w01), dotw(w67, w45)
    w03, w47 = wide(m03), wide(m47)
    total = dotw(w47, w03)
    w27 = wide(dotw(w47, w23))
    after = [dotw(w27, w[1]), None, dotw(w47, w[3]), None, dotw(w67, w[5])]
    after = [wide(after[0]), w27, wide(after[2]), w47, wide(after[4]), w67, w[7]]
    return total, after, (w, w01, w23, w45, w03)


def before(ws):
    w, w01, w23, w45, w03 = ws
    w6 = wide(dotw(w45, w03))
    return [w[0], w01, wide(dotw(w[2], w01)), w03, wide(dotw(w[4], w03)), w6, wide(dotw(w[6], w6))]


def added(a, get):
    a01 = dotw(get("1"), wide(a[0])) + a[1]
    a23 = dotw(get("3"), wide(a[2])) + a[3]
    a45 = dotw(get("5"), wide(a[4])) + a[5]
    w01 = wide(a01)
    a03 = dotw(get("23"), w01) + a23
    w03 = wide(a03)
    a6 = dotw(get("45"), w03) + a45
    return [
        a[0], a01, dotw(get("2"), w01) + a[2], a03, dotw(get("4"), w03) + a[4], a6,
        dotw(get("6"), wide(a6)) + a[6],
    ]


def total_added(after, a):
    t = a[7]
    for i in range(7):
        t = t + dotw(after[i], wide(a[i]))
    return t


NAMES = {"1": 0, "2": 1, "3": 2, "4": 3, "5": 4, "6": 5, "23": 6, "45": 7}


def keep_products(ref, ws):
    w, w01, w23, w45, w03 = ws
    for name, x in zip(NAMES, [w[1], w[2], w[3], w[4], w[5], w[6], w23, w45]):
        ref[NAMES[name]] = x


def iota(shape, dim):
    return lax.broadcasted_iota(jnp.int32, shape, dim)


SIZES = (8, 16, 32, 64)


def stack_parts(x):
    hi = x.astype(BF16).astype(F32)
    return jnp.concatenate([hi, x - hi], 0).astype(BF16)


def dot_stacked(a, b):
    m, n = a.shape[0] // 2, b.shape[1] // 2
    r = dotf(a, b)
    return r[:m, :n] + (r[m:, :n] + r[:m, n:])


def invert(lows):
    row, col = iota((B, B), 0), iota((B, B), 1)
    n = len(lows)
    near = (row // 8) == (col // 8)
    parts = [
        stack_parts(jnp.sum(jnp.where(near, low, 0.0).reshape(16, 8, B), axis=0)) for low in lows
    ]
    lsp = [jnp.concatenate(split(low), 1) for low in lows]
    stacked = jnp.concatenate(parts, 0)
    spread = []
    for m in range(7):
        pick = jnp.where(near & (row % 8 == m), 1.0, 0.0).astype(BF16)
        r = dotf(stacked, pick).reshape(n, 2, 8, B)
        spread.append(r[:, 0] + r[:, 1])
    inv = jnp.broadcast_to((iota((8, B), 1) % 8 == iota((8, B), 0)).astype(F32), (n, 8, B))
    for m in range(7):
        inv = inv - spread[m] * inv[:, m : m + 1]
    inv = [inv[s] for s in range(n)]
    row2, col2 = iota((B, 2 * B), 0), iota((B, 2 * B), 1) % B
    for size in SIZES:
        below = (row2 // size == col2 // size + 1) & (row2 // size % 2 == 1)
        same = row2 // size == col2 // size
        odd = iota((size, B), 1) // size % 2 == 1
        xs, tops = [], []
        for s in range(n):
            upper = jnp.where(odd, 0.0, inv[s])
            inv[s] = jnp.where(odd, inv[s], 0.0)
            tops.append(upper)
            low = jnp.where(below, lsp[s], jnp.zeros_like(lsp[s]))
            xs.append(dot_stacked(stack_parts(inv[s]), low))
        for s in range(n):
            two = [tops[s]] * (16 // size if size < 16 else 1)
            two = jnp.concatenate(two, 0) if len(two) > 1 else two[0]
            wide = jnp.concatenate(split(two), 1)
            wide = jnp.concatenate([wide] * (B // wide.shape[0]), 0)
            wide = jnp.where(same, wide, jnp.zeros_like(wide))
            y = dot_stacked(stack_parts(xs[s]), wide)
            inv[s] = jnp.concatenate([tops[s], inv[s] - y], 0)
    return inv


def kernel(
    doc_ref, q_hbm, k_hbm, v_hbm, rate_hbm, gain_hbm, o_ref,
    q_ref, k_ref, v_ref, rate_ref, gain_ref, cols_ref, scale_ref, wu_ref, bm_ref, prod_ref, add_ref, mat_ref, got_ref, ybuf_ref, ysend_ref, pz_ref, pa_ref, oprod_ref, oafter_ref,
    sout_ref, sbuf_ref, qp_ref, o1_ref, xsend_ref, xbuf_ref,
    in_sem, g_send, g_recv, y_send, y_recv, s_send, s_recv, x_send, x_recv,
):
    def load(i, hbm, ref, h):
        if h is not None:
            hbm, ref = hbm.at[:, h * B : h * B + B], ref.at[:, h * B : h * B + B]
        return pltpu.make_async_copy(hbm, ref, in_sem.at[i])

    loads = [
        load(0, rate_hbm, rate_ref, None),
        load(1, k_hbm, k_ref, 0),
        load(2, v_hbm, v_ref, 0),
        load(3, k_hbm, k_ref, 1),
        load(4, v_hbm, v_ref, 1),
        load(5, gain_hbm, gain_ref, None),
        load(6, q_hbm, q_ref, None),
    ]
    for copy in loads:
        copy.start()
    ctx, head = lax.axis_index("ctx"), lax.axis_index("head")
    y, z = ctx // ROWS, lax.rem(ctx, ROWS)
    core = lax.rem(head, 2)

    def at_z(other):
        return {"ctx": y * ROWS + other}

    def at_y(other):
        return {"ctx": lax.rem(other, 4) * ROWS + z}

    def owner_z(h):
        return 4 * core + 2 * h

    mine = (z // 4 == core) & (lax.rem(z, 2) == 0)
    my_h = lax.rem(z, 4) // 2

    barrier = pltpu.get_barrier_semaphore()
    for i in range(1, ROWS):
        pl.semaphore_signal(barrier, 1, device_id=at_z(lax.rem(z + i, ROWS)), device_id_type=MESH)
    for i in range(1, 4):
        pl.semaphore_signal(barrier, 1, device_id=at_y(y + i), device_id_type=MESH)
    for i in range(1, 8):
        pl.semaphore_signal(barrier, 1, device_id={"head": lax.rem(head + i, 8)}, device_id_type=MESH)

    base = ctx * (NB * B)
    pos = base + iota((NB, B), 0) * B + iota((NB, B), 1)
    begin = jnp.int32(0)
    start = jnp.zeros((NB, B), jnp.int32)
    for m in range(31):
        begin = begin + doc_ref[m]
        start = jnp.where(pos >= begin, begin, start)
    loads[0].wait()
    rates = [rate_ref[h : h + 1, b * B : b * B + B] for h in range(2) for b in range(NB)]
    start_f = (start - base).astype(F32)
    cols_ref[...] = jnp.concatenate([start_f] + rates + [start_f] * 13, 0).T

    row, col = iota((B, B), 0), iota((B, B), 1)
    eye = (row == col).astype(F32)
    row1 = iota((B, 1), 0).astype(F32)
    colf = col.astype(F32)

    def doc_columns(b):
        first = cols_ref[:, b : b + 1]
        carry = (first < float(b * B)).astype(F32)
        last = (row1 + float(b * B) >= first[B - 1 : B]).astype(F32)
        return first, carry, last

    def lanes(h):
        return pl.ds(pl.multiple_of(h * B, B), B)

    def rate(b, h):
        i = NB + h * NB + b
        return cols_ref[:, i : i + 1]

    def own_product(h):
        lows, rights, scales = [], [], []
        for b in range(NB):
            kb = k_ref[pl.ds(b * B, B), lanes(h)]
            kf = kb.astype(F32)
            rk = lax.rsqrt(jnp.sum(kf * kf, axis=1, keepdims=True) + EPS)
            first, _, _ = doc_columns(b)
            keep = (row > col) & (colf + float(b * B) >= first)
            scale = rate(b, h) * rk
            scales.append(scale)
            lows.append(jnp.where(keep, dot_nt(kb, kb) * (scale * rk), 0.0))
            rights.append(wide(kf * (scale * rk)))
        inv = [wide(t) for t in invert(lows)]
        ws = [dotw(inv[b], rights[b]) for b in range(NB)]
        ms, kts = [], []
        for b in range(NB):
            _, carry, last = doc_columns(b)
            w = ws[b] * carry
            wu_ref[h, b, :, :B] = w
            hi, lo = split(w * last)
            kt = k_ref[pl.ds(b * B, B), lanes(h)].T
            kts.append(jnp.concatenate([kt, kt], 1))
            m = dotf(kts[b], jnp.concatenate([hi, lo], 0))
            ms.append(jnp.where(row == col, carry[B - 1 : B], 0.0) - m)
        total, after, some = products(ms)
        mat_ref[h, 0] = total
        return inv, scales, kts, after, some

    def own_added(h, inv, scales, kts, after):
        us = []
        for b in range(NB):
            vf = v_ref[pl.ds(b * B, B), lanes(h)].astype(F32)
            us.append(dotw(inv[b], wide(vf * scales[b])))
        adds = []
        for b in range(NB):
            _, _, last = doc_columns(b)
            wu_ref[h, b, :, B:] = us[b]
            hi, lo = split(us[b] * last)
            adds.append(dotf(kts[b], jnp.concatenate([hi, lo], 0)))
            add_ref[h, b] = adds[b]
        mat_ref[h, 1] = total_added(after, adds)

    def send_map(h, part):
        return pltpu.make_async_remote_copy(
            src_ref=mat_ref.at[h, part], dst_ref=got_ref.at[z, part],
            send_sem=g_send.at[h, part], recv_sem=g_recv.at[z, part],
            device_id=at_z(owner_z(h)), device_id_type=MESH,
        )

    def give(h, part):
        @pl.when(z != owner_z(h))
        def _():
            send_map(h, part).start()

        @pl.when(z == owner_z(h))
        def _():
            got_ref[z, part] = mat_ref[h, part]

    @pl.when(y < 2)
    def _():
        ybuf_ref[0] = jnp.zeros((B, B), F32)
        ybuf_ref[2] = jnp.zeros((B, B), F32)

    @pl.when(y == 0)
    def _():
        ybuf_ref[1] = jnp.zeros((B, B), F32)

    left = []
    for h in range(2):
        loads[1 + 2 * h].wait()
        left.append(own_product(h))
        if h == 0:
            pl.semaphore_wait(barrier, 17)
        give(h, 0)
    for h in range(2):
        loads[2 + 2 * h].wait()
        own_added(h, *left[h][:4])
        give(h, 1)
    for h in range(2):
        keep_products(prod_ref.at[h], left[h][4])
        for i, x in enumerate(before(left[h][4])):
            bm_ref[h, i] = x

    def shadow(h):
        adds = added([add_ref[h, b] for b in range(NB)], lambda name: prod_ref[h, NAMES[name]])
        scores, lefts = [], []
        for b in range(NB):
            kb = k_ref[pl.ds(b * B, B), lanes(h)]
            qb = q_ref[pl.ds(b * B, B), lanes(h)]
            qf = qb.astype(F32)
            rq = lax.rsqrt(jnp.sum(qf * qf, axis=1, keepdims=True) + EPS)
            first, carry, _ = doc_columns(b)
            keep = (row >= col) & (colf + float(b * B) >= first)
            scores.append(jnp.where(keep, dot_nt(qb, kb) * rq, 0.0))
            lefts.append(qf * (rq * carry))
        both = [dot3(split(scores[b]), split(wu_ref[h, b])) for b in range(NB)]
        qes = [lefts[b] - both[b][:, :B] for b in range(NB)]
        o1s = [both[b][:, B:] for b in range(NB)]
        qxs = []
        for b in range(1, NB):
            bm, (ah, al) = bm_ref[h, b - 1], split(adds[b - 1])
            right = (
                jnp.concatenate([bm[:, :B], ah], 1),
                jnp.concatenate([bm[:, B:], al], 1),
            )
            qxs.append(dot3(split(qes[b]), right))
        for b in range(NB):
            qe, o1 = qes[b], o1s[b]
            if b > 0:
                qe, o1 = qxs[b - 1][:, :B], o1 + qxs[b - 1][:, B:]
            hi, lo = split(qe)
            qp_ref[h, pl.ds(b * B, B)] = jnp.concatenate([hi, lo], 1)
            o1_ref[h, pl.ds(b * B, B)] = o1

    loads[5].wait()
    loads[6].wait()
    for h in range(2):
        shadow(h)

    def send_y(src, slot, step):
        return pltpu.make_async_remote_copy(
            src_ref=ysend_ref.at[src], dst_ref=ybuf_ref.at[slot],
            send_sem=y_send.at[slot], recv_sem=y_recv.at[slot],
            device_id=at_y(y + step), device_id_type=MESH,
        )

    def send_state(i):
        to = lax.rem(z + i, ROWS)
        return pltpu.make_async_remote_copy(
            src_ref=sout_ref.at[to], dst_ref=sbuf_ref.at[my_h],
            send_sem=s_send.at[to], recv_sem=s_recv.at[my_h],
            device_id=at_z(to), device_id_type=MESH,
        )

    def wait_maps(part):
        for i in range(1, ROWS):
            frm = lax.rem(z + i, ROWS)
            pltpu.make_async_remote_copy(
                src_ref=mat_ref.at[0, part], dst_ref=got_ref.at[frm, part],
                send_sem=g_send.at[0, part], recv_sem=g_recv.at[frm, part],
                device_id=at_z(frm), device_id_type=MESH,
            ).wait_recv()

    @pl.when(mine)
    def _():
        wait_maps(0)
        total, after, some = products([got_ref[i, 0] for i in range(ROWS)])
        ysend_ref[0] = total
        @pl.when((y == 1) | (y == 2))
        def _():
            send_y(0, 0, 1).start()

        keep_products(oprod_ref, some)
        pz_ref[0] = jnp.concatenate([eye, jnp.zeros_like(eye)], 1).astype(BF16)
        for i, x in enumerate(before(some)):
            pz_ref[i + 1] = x
        for i, x in enumerate(after):
            oafter_ref[i] = x
        wait_maps(1)
        states = [got_ref[i, 1] for i in range(ROWS)]
        ysend_ref[1] = total_added([oafter_ref[i] for i in range(7)], states)
        @pl.when(y <= 2)
        def _():
            send_y(1, 1, 1).start()

        @pl.when(y <= 1)
        def _():
            send_y(1, 2, 2).start()

        pa_ref[0] = jnp.zeros((B, B), F32)
        for i, x in enumerate(added(states, lambda name: oprod_ref[NAMES[name]])):
            pa_ref[i + 1] = x
        @pl.when(y >= 1)
        def _():
            send_y(1, 1, 1).wait_recv()

        @pl.when(y >= 2)
        def _():
            send_y(0, 0, 1).wait_recv()
            send_y(1, 2, 2).wait_recv()

        s_row = ybuf_ref[1] + dotw(wide(ybuf_ref[0]), wide(ybuf_ref[2]))
        sh, sl = split(s_row)
        shh = jnp.concatenate([sh, sh], 0)
        for i in (4, 3, 5, 2, 6, 1, 7, 0):
            to = lax.rem(z + i, ROWS)
            pm = pz_ref[to]
            sout_ref[to] = pa_ref[to] + dotf(pm, shh) + dotf(pm[:, :B], sl)
            if i:
                send_state(i).start()
        sbuf_ref[my_h] = sout_ref[z]

    for h in range(2):

        @pl.when(z != owner_z(h))
        def _():
            pltpu.make_async_remote_copy(
                src_ref=sout_ref.at[0], dst_ref=sbuf_ref.at[h],
                send_sem=s_send.at[0], recv_sem=s_recv.at[h],
                device_id=at_z(owner_z(h)), device_id_type=MESH,
            ).wait_recv()

    squares = [None] * NB
    for h in range(2):
        sh, sl = split(sbuf_ref[h])
        shh = jnp.concatenate([sh, sh], 0)
        for b in range(NB):
            rows = pl.ds(b * B, B)
            qp = qp_ref[h, rows]
            o = o1_ref[h, rows] + dotf(qp, shh) + dotf(qp[:, :B], sl)
            o1_ref[h, rows] = o
            squares[b] = o * o if h == 0 else squares[b] + o * o
    ones = jnp.ones((8, B), BF16)
    sub = iota((8, B), 0)
    sums = jnp.zeros((8, B), F32)
    for b in range(NB):
        hi, lo = split(squares[b])
        sums = jnp.where(sub == b, dot_nt(ones, hi) + dot_nt(ones, lo), sums)
    xsend_ref[...] = sums

    def send_x(i):
        return pltpu.make_async_remote_copy(
            src_ref=xsend_ref, dst_ref=xbuf_ref.at[i - 1],
            send_sem=x_send.at[i - 1], recv_sem=x_recv.at[i - 1],
            device_id={"head": lax.rem(head + i, 8)}, device_id_type=MESH,
        )

    for i in range(1, 8):
        send_x(i).start()
    for i in range(1, 8):
        send_x(i).wait()
        sums = sums + xbuf_ref[i - 1]
    scale = lax.rsqrt(sums / WIDTH + EPS)
    scale_ref[...] = jnp.concatenate([scale] * 16, 0).T
    for h in range(2):
        gain = gain_ref[:, h * B : h * B + B]
        for b in range(NB):
            rows = pl.ds(b * B, B)
            o_ref[rows, h * B : h * B + B] = (
                o1_ref[h, rows] * scale_ref[:, b : b + 1] * gain
            ).astype(BF16)

    for h in range(2):

        @pl.when(z != owner_z(h))
        def _():
            send_map(h, 0).wait_send()
            send_map(h, 1).wait_send()

    @pl.when(mine)
    def _():
        for i in range(1, ROWS):
            send_state(i).wait_send()

        @pl.when((y == 1) | (y == 2))
        def _():
            send_y(0, 0, 1).wait_send()

        @pl.when(y <= 2)
        def _():
            send_y(1, 1, 1).wait_send()

        @pl.when(y <= 1)
        def _():
            send_y(1, 2, 2).wait_send()


def local(queries, key_vectors, value_vectors, write_rates, doc_lengths, norm_gain):
    vm = pl.BlockSpec(memory_space=pltpu.VMEM)
    return pl.pallas_call(
        kernel,
        out_shape=pltpu.VMEM(queries.shape, BF16),
        in_specs=[pl.BlockSpec(memory_space=pltpu.SMEM)]
        + [pl.BlockSpec(memory_space=pltpu.HBM)] * 5,
        out_specs=vm,
        scratch_shapes=[
            pltpu.VMEM((NB * B, 2 * B), BF16),
            pltpu.VMEM((NB * B, 2 * B), BF16),
            pltpu.VMEM((NB * B, 2 * B), BF16),
            pltpu.VMEM((2, NB * B), F32),
            pltpu.VMEM((1, 2 * B), F32),
            pltpu.VMEM((B, B), F32),
            pltpu.VMEM((B, B), F32),
            pltpu.VMEM((2, NB, B, 2 * B), F32),
            pltpu.VMEM((2, 7, B, 2 * B), BF16),
            pltpu.VMEM((2, 8, B, 2 * B), BF16),
            pltpu.VMEM((2, NB, B, B), F32),
            pltpu.VMEM((2, 2, B, B), F32),
            pltpu.VMEM((ROWS, 2, B, B), F32),
            pltpu.VMEM((3, B, B), F32),
            pltpu.VMEM((2, B, B), F32),
            pltpu.VMEM((ROWS, B, 2 * B), BF16),
            pltpu.VMEM((ROWS, B, B), F32),
            pltpu.VMEM((8, B, 2 * B), BF16),
            pltpu.VMEM((7, B, 2 * B), BF16),
            pltpu.VMEM((ROWS, B, B), F32),
            pltpu.VMEM((2, B, B), F32),
            pltpu.VMEM((2, NB * B, 2 * B), BF16),
            pltpu.VMEM((2, NB * B, B), F32),
            pltpu.VMEM((8, B), F32),
            pltpu.VMEM((7, 8, B), F32),
            pltpu.SemaphoreType.DMA((7,)),
            pltpu.SemaphoreType.DMA((2, 2)),
            pltpu.SemaphoreType.DMA((ROWS, 2)),
            pltpu.SemaphoreType.DMA((3,)),
            pltpu.SemaphoreType.DMA((3,)),
            pltpu.SemaphoreType.DMA((ROWS,)),
            pltpu.SemaphoreType.DMA((2,)),
            pltpu.SemaphoreType.DMA((7,)),
            pltpu.SemaphoreType.DMA((7,)),
        ],
        compiler_params=pltpu.CompilerParams(
            collective_id=0, has_side_effects=True, vmem_limit_bytes=63 << 20
        ),
    )(doc_lengths, queries, key_vectors, value_vectors, write_rates.T, norm_gain[None])


def solution(mesh):
    tokens = P("ctx", "head")
    return jax.shard_map(
        local, mesh=mesh, in_specs=(tokens,) * 4 + (P(), P("head")), out_specs=tokens,
        check_vma=False,
    )
```

```python
import functools

import jax
import jax.numpy as jnp
from jax import lax
from jax.experimental import pallas as pl
from jax.experimental.pallas import tpu as pltpu
from jax.sharding import PartitionSpec as P

MESH = pl.DeviceIdType.MESH
F32, BF16 = jnp.float32, jnp.bfloat16
EPS = 1e-6
B = 128
NB = 8
ROWS = 8
WIDTH = 2048


def dotf(a, b):
    return lax.dot_general(a, b, (((1,), (0,)), ((), ())), preferred_element_type=F32)


def dot_nt(a, b):
    return lax.dot_general(a, b, (((1,), (1,)), ((), ())), preferred_element_type=F32)


def dot_tn(a, b):
    return lax.dot_general(a, b, (((0,), (0,)), ((), ())), preferred_element_type=F32)


def split(x):
    hi = x.astype(BF16)
    return hi, (x - hi.astype(F32)).astype(BF16)


def dot3(a, b):
    (ah, al), (bh, bl) = a, b
    return dotf(jnp.concatenate([ah, al], 1), jnp.concatenate([bh, bh], 0)) + dotf(ah, bl)


def wide(x):
    return jnp.concatenate(split(x), 1)


def dotw(a, b):
    n = b.shape[1] // 2
    r = dotf(a, jnp.concatenate([b, b], 0))
    return r[:, :n] + r[:, n:]


def products(ms):
    w = [wide(m) for m in ms]
    m01, m23, m45, m67 = [dotw(w[i + 1], w[i]) for i in range(0, 8, 2)]
    w01, w23, w45, w67 = [wide(m) for m in (m01, m23, m45, m67)]
    m03, m47 = dotw(w23, w01), dotw(w67, w45)
    w03, w47 = wide(m03), wide(m47)
    total = dotw(w47, w03)
    w27 = wide(dotw(w47, w23))
    after = [dotw(w27, w[1]), None, dotw(w47, w[3]), None, dotw(w67, w[5])]
    after = [wide(after[0]), w27, wide(after[2]), w47, wide(after[4]), w67, w[7]]
    return total, after, (w, w01, w23, w45, w03)


def before(ws):
    w, w01, w23, w45, w03 = ws
    w6 = wide(dotw(w45, w03))
    return [w[0], w01, wide(dotw(w[2], w01)), w03, wide(dotw(w[4], w03)), w6, wide(dotw(w[6], w6))]


def added(a, get):
    a01 = dotw(get("1"), wide(a[0])) + a[1]
    a23 = dotw(get("3"), wide(a[2])) + a[3]
    a45 = dotw(get("5"), wide(a[4])) + a[5]
    w01 = wide(a01)
    a03 = dotw(get("23"), w01) + a23
    w03 = wide(a03)
    a6 = dotw(get("45"), w03) + a45
    return [
        a[0], a01, dotw(get("2"), w01) + a[2], a03, dotw(get("4"), w03) + a[4], a6,
        dotw(get("6"), wide(a6)) + a[6],
    ]


def total_added(after, a):
    t = a[7]
    for i in range(7):
        t = t + dotw(after[i], wide(a[i]))
    return t


NAMES = {"1": 0, "2": 1, "3": 2, "4": 3, "5": 4, "6": 5, "23": 6, "45": 7}


def keep_products(ref, ws):
    w, w01, w23, w45, w03 = ws
    for name, x in zip(NAMES, [w[1], w[2], w[3], w[4], w[5], w[6], w23, w45]):
        ref[NAMES[name]] = x


def iota(shape, dim):
    return lax.broadcasted_iota(jnp.int32, shape, dim)


SIZES = (8, 16, 32, 64)


def stack_parts(x):
    hi = x.astype(BF16).astype(F32)
    return jnp.concatenate([hi, x - hi], 0).astype(BF16)


def dot_stacked(a, b):
    m, n = a.shape[0] // 2, b.shape[1] // 2
    r = dotf(a, b)
    return r[:m, :n] + (r[m:, :n] + r[:m, n:])


def invert(lows):
    row, col = iota((B, B), 0), iota((B, B), 1)
    n = len(lows)
    near = (row // 8) == (col // 8)
    parts = [
        stack_parts(jnp.sum(jnp.where(near, low, 0.0).reshape(16, 8, B), axis=0)) for low in lows
    ]
    lsp = [jnp.concatenate(split(low), 1) for low in lows]
    stacked = jnp.concatenate(parts, 0)
    spread = []
    for m in range(7):
        pick = jnp.where(near & (row % 8 == m), 1.0, 0.0).astype(BF16)
        r = dotf(stacked, pick).reshape(n, 2, 8, B)
        spread.append(r[:, 0] + r[:, 1])
    inv = jnp.broadcast_to((iota((8, B), 1) % 8 == iota((8, B), 0)).astype(F32), (n, 8, B))
    for m in range(7):
        inv = inv - spread[m] * inv[:, m : m + 1]
    inv = [inv[s] for s in range(n)]
    row2, col2 = iota((B, 2 * B), 0), iota((B, 2 * B), 1) % B
    for size in SIZES:
        below = (row2 // size == col2 // size + 1) & (row2 // size % 2 == 1)
        same = row2 // size == col2 // size
        odd = iota((size, B), 1) // size % 2 == 1
        xs, tops = [], []
        for s in range(n):
            upper = jnp.where(odd, 0.0, inv[s])
            inv[s] = jnp.where(odd, inv[s], 0.0)
            tops.append(upper)
            low = jnp.where(below, lsp[s], jnp.zeros_like(lsp[s]))
            xs.append(dot_stacked(stack_parts(inv[s]), low))
        for s in range(n):
            two = [tops[s]] * (16 // size if size < 16 else 1)
            two = jnp.concatenate(two, 0) if len(two) > 1 else two[0]
            wide = jnp.concatenate(split(two), 1)
            wide = jnp.concatenate([wide] * (B // wide.shape[0]), 0)
            wide = jnp.where(same, wide, jnp.zeros_like(wide))
            y = dot_stacked(stack_parts(xs[s]), wide)
            inv[s] = jnp.concatenate([tops[s], inv[s] - y], 0)
    return inv


def kernel(
    doc_ref, q_hbm, k_hbm, v_hbm, rate_hbm, gain_hbm, o_ref,
    q_ref, k_ref, v_ref, rate_ref, gain_ref, cols_ref, end_ref, scale_ref, wu_ref, prod_ref, add_ref, mat_ref, got_ref, ybuf_ref, ysend_ref, pz_ref, pa_ref, oprod_ref, oafter_ref,
    sout_ref, sbuf_ref, qp_ref, o1_ref, xsend_ref, xbuf_ref,
    in_sem, g_send, g_recv, y_send, y_recv, s_send, s_recv, x_send, x_recv,
):
    def load(i, hbm, ref, h):
        if h is not None:
            hbm, ref = hbm.at[:, h * B : h * B + B], ref.at[:, h * B : h * B + B]
        return pltpu.make_async_copy(hbm, ref, in_sem.at[i])

    loads = [
        load(0, rate_hbm, rate_ref, None),
        load(1, k_hbm, k_ref, 0),
        load(2, v_hbm, v_ref, 0),
        load(3, k_hbm, k_ref, 1),
        load(4, v_hbm, v_ref, 1),
        load(5, gain_hbm, gain_ref, None),
        load(6, q_hbm, q_ref, None),
    ]
    for i in (1, 0, 3, 2, 4, 5, 6):
        loads[i].start()
    ctx, head = lax.axis_index("ctx"), lax.axis_index("head")
    y, z = ctx // ROWS, lax.rem(ctx, ROWS)
    core = lax.rem(head, 2)

    def at_z(other):
        return {"ctx": y * ROWS + other}

    def at_y(other):
        return {"ctx": lax.rem(other, 4) * ROWS + z}

    def owner_z(h):
        return 4 * core + 2 * h

    mine = (z // 4 == core) & (lax.rem(z, 2) == 0)
    my_h = lax.rem(z, 4) // 2

    barrier = pltpu.get_barrier_semaphore()
    for i in range(1, ROWS):
        pl.semaphore_signal(barrier, 1, device_id=at_z(lax.rem(z + i, ROWS)), device_id_type=MESH)
    for i in range(1, 4):
        pl.semaphore_signal(barrier, 1, device_id=at_y(y + i), device_id_type=MESH)
    for i in range(1, 8):
        pl.semaphore_signal(barrier, 1, device_id={"head": lax.rem(head + i, 8)}, device_id_type=MESH)

    base = ctx * (NB * B)
    pos = base + iota((NB, B), 0) * B + iota((NB, B), 1)
    begin = jnp.int32(0)
    start = jnp.zeros((NB, B), jnp.int32)
    end = jnp.full((NB, B), doc_ref[0])
    for m in range(31):
        begin = begin + doc_ref[m]
        passed = pos >= begin
        start = jnp.where(passed, begin, start)
        end = jnp.where(passed, begin + doc_ref[m + 1], end)
    end_ref[...] = (end - base - iota((NB, B), 0) * B).astype(F32)
    loads[0].wait()
    rates = [rate_ref[h : h + 1, b * B : b * B + B] for h in range(2) for b in range(NB)]
    start_f = (start - base).astype(F32)
    cols_ref[...] = jnp.concatenate([start_f] + rates + [start_f] * 13, 0).T

    row, col = iota((B, B), 0), iota((B, B), 1)
    eye = (row == col).astype(F32)
    rowf = row.astype(F32)
    ones2 = jnp.ones((2 * B, B), BF16)

    def same_doc(b):
        return rowf < end_ref[b : b + 1]

    def carried(b):
        return (cols_ref[:, b : b + 1] < float(b * B)).astype(F32)

    def unbroken(b):
        return (cols_ref[B - 1 : B, b : b + 1] < float(b * B)).astype(F32)

    def last_keys(b, kt):
        return jnp.where(end_ref[b : b + 1] >= float(B), kt.astype(F32), 0.0).astype(BF16)

    def norms(x):
        return lax.rsqrt(dotf(wide(x * x), ones2) + EPS)

    def lanes(h):
        return pl.ds(pl.multiple_of(h * B, B), B)

    def rate(b, h):
        i = NB + h * NB + b
        return cols_ref[:, i : i + 1]

    def own_product(h):
        lows, rights, scales = [], [], []
        for b in range(NB):
            kb = k_ref[pl.ds(b * B, B), lanes(h)]
            kf = kb.astype(F32)
            rk = norms(kf)
            keep = (row > col) & same_doc(b)
            scale = rate(b, h) * rk
            scales.append(scale)
            lows.append(jnp.where(keep, dot_nt(kb, kb) * (scale * rk), 0.0))
            rights.append(wide(kf * (scale * rk)))
        inv = [wide(t) for t in invert(lows)]
        ws = [dotw(inv[b], rights[b]) for b in range(NB)]
        ms, kts = [], []
        for b in range(NB):
            wu_ref[h, b, :, :B] = ws[b]
            kt = k_ref[pl.ds(b * B, B), lanes(h)].T
            m = dotf(jnp.concatenate([kt, kt], 1), jnp.concatenate(split(ws[b]), 0))
            ms.append((eye - m) * unbroken(b))
            kts.append(kt)
        total, after, some = products(ms)
        mat_ref[h, 0] = total
        return inv, scales, kts, after, some

    def own_added(h, inv, scales, kts, after):
        us = []
        for b in range(NB):
            vf = v_ref[pl.ds(b * B, B), lanes(h)].astype(F32)
            us.append(dotw(inv[b], wide(vf * scales[b])))
        adds = []
        for b in range(NB):
            wu_ref[h, b, :, B:] = us[b]
            kt = last_keys(b, kts[b])
            adds.append(dotf(jnp.concatenate([kt, kt], 1), jnp.concatenate(split(us[b]), 0)))
            add_ref[h, b] = adds[b]
        mat_ref[h, 1] = total_added(after, adds)

    def send_map(h, part):
        return pltpu.make_async_remote_copy(
            src_ref=mat_ref.at[h, part], dst_ref=got_ref.at[z, part],
            send_sem=g_send.at[h, part], recv_sem=g_recv.at[z, part],
            device_id=at_z(owner_z(h)), device_id_type=MESH,
        )

    def give(h, part):
        @pl.when(z != owner_z(h))
        def _():
            send_map(h, part).start()

        @pl.when(z == owner_z(h))
        def _():
            got_ref[z, part] = mat_ref[h, part]

    @pl.when(y < 2)
    def _():
        ybuf_ref[0] = jnp.zeros((B, B), F32)
        ybuf_ref[2] = jnp.zeros((B, B), F32)

    @pl.when(y == 0)
    def _():
        ybuf_ref[1] = jnp.zeros((B, B), F32)

    loads[1].wait()
    left = [own_product(0)]
    pl.semaphore_wait(barrier, 17)
    give(0, 0)
    loads[3].wait()
    left.append(own_product(1))
    give(1, 0)
    loads[2].wait()
    loads[4].wait()
    own_added(0, *left[0][:4])
    own_added(1, *left[1][:4])
    give(0, 1)
    give(1, 1)

    def shadow(h):
        keep_products(prod_ref.at[h], left[h][4])
        bms = before(left[h][4])
        adds = added([add_ref[h, b] for b in range(NB)], lambda name: prod_ref[h, NAMES[name]])
        scores, lefts = [], []
        for b in range(NB):
            kb = k_ref[pl.ds(b * B, B), lanes(h)]
            qb = q_ref[pl.ds(b * B, B), lanes(h)]
            qf = qb.astype(F32)
            rq = norms(qf)
            keep = (row >= col) & same_doc(b)
            scores.append(jnp.where(keep, dot_nt(qb, kb) * rq, 0.0))
            lefts.append(qf * rq)
        both = [dot3(split(scores[b]), split(wu_ref[h, b])) for b in range(NB)]
        qes = [(lefts[b] - both[b][:, :B]) * carried(b) for b in range(NB)]
        o1s = [both[b][:, B:] for b in range(NB)]
        qxs = []
        for b in range(1, NB):
            bm, (ah, al) = bms[b - 1], split(adds[b - 1])
            right = (
                jnp.concatenate([bm[:, :B], ah], 1),
                jnp.concatenate([bm[:, B:], al], 1),
            )
            qxs.append(dot3(split(qes[b]), right))
        for b in range(NB):
            qe, o1 = qes[b], o1s[b]
            if b > 0:
                qe, o1 = qxs[b - 1][:, :B], o1 + qxs[b - 1][:, B:]
            hi, lo = split(qe)
            qp_ref[h, pl.ds(b * B, B)] = jnp.concatenate([hi, lo], 1)
            o1_ref[h, pl.ds(b * B, B)] = o1

    loads[5].wait()
    loads[6].wait()
    shadow(0)
    def send_y(src, slot, step):
        return pltpu.make_async_remote_copy(
            src_ref=ysend_ref.at[src], dst_ref=ybuf_ref.at[slot],
            send_sem=y_send.at[slot], recv_sem=y_recv.at[slot],
            device_id=at_y(y + step), device_id_type=MESH,
        )

    def send_state(i):
        to = lax.rem(z + i, ROWS)
        return pltpu.make_async_remote_copy(
            src_ref=sout_ref.at[to], dst_ref=sbuf_ref.at[my_h],
            send_sem=s_send.at[to], recv_sem=s_recv.at[my_h],
            device_id=at_z(to), device_id_type=MESH,
        )

    def wait_maps(part):
        for i in range(1, ROWS):
            frm = lax.rem(z + i, ROWS)
            pltpu.make_async_remote_copy(
                src_ref=mat_ref.at[0, part], dst_ref=got_ref.at[frm, part],
                send_sem=g_send.at[0, part], recv_sem=g_recv.at[frm, part],
                device_id=at_z(frm), device_id_type=MESH,
            ).wait_recv()

    @pl.when(mine)
    def _():
        wait_maps(0)
        total, after, some = products([got_ref[i, 0] for i in range(ROWS)])
        ysend_ref[0] = total
        @pl.when((y == 1) | (y == 2))
        def _():
            send_y(0, 0, 1).start()

        keep_products(oprod_ref, some)
        pz_ref[0] = jnp.concatenate([eye, jnp.zeros_like(eye)], 1).astype(BF16)
        for i, x in enumerate(before(some)):
            pz_ref[i + 1] = x
        for i, x in enumerate(after):
            oafter_ref[i] = x
        wait_maps(1)
        states = [got_ref[i, 1] for i in range(ROWS)]
        ysend_ref[1] = total_added([oafter_ref[i] for i in range(7)], states)
        @pl.when(y <= 2)
        def _():
            send_y(1, 1, 1).start()

        @pl.when(y <= 1)
        def _():
            send_y(1, 2, 2).start()

    shadow(1)

    @pl.when(mine)
    def _():
        states = [got_ref[i, 1] for i in range(ROWS)]
        pa_ref[0] = jnp.zeros((B, B), F32)
        for i, x in enumerate(added(states, lambda name: oprod_ref[NAMES[name]])):
            pa_ref[i + 1] = x
        @pl.when(y >= 1)
        def _():
            send_y(1, 1, 1).wait_recv()

        @pl.when(y >= 2)
        def _():
            send_y(0, 0, 1).wait_recv()
            send_y(1, 2, 2).wait_recv()

        s_row = ybuf_ref[1] + dotw(wide(ybuf_ref[0]), wide(ybuf_ref[2]))
        sh, sl = split(s_row)
        shh = jnp.concatenate([sh, sh], 0)
        for i in (4, 3, 5, 2, 6, 1, 7, 0):
            to = lax.rem(z + i, ROWS)
            pm = pz_ref[to]
            sout_ref[to] = pa_ref[to] + dotf(pm, shh) + dotf(pm[:, :B], sl)
            if i:
                send_state(i).start()
        sbuf_ref[my_h] = sout_ref[z]

    for h in range(2):

        @pl.when(z != owner_z(h))
        def _():
            pltpu.make_async_remote_copy(
                src_ref=sout_ref.at[0], dst_ref=sbuf_ref.at[h],
                send_sem=s_send.at[0], recv_sem=s_recv.at[h],
                device_id=at_z(owner_z(h)), device_id_type=MESH,
            ).wait_recv()

    squares = [None] * NB
    for h in range(2):
        sh, sl = split(sbuf_ref[h])
        shh = jnp.concatenate([sh, sh], 0)
        for b in range(NB):
            rows = pl.ds(b * B, B)
            qp = qp_ref[h, rows]
            o = o1_ref[h, rows] + dotf(qp, shh) + dotf(qp[:, :B], sl)
            o1_ref[h, rows] = o
            squares[b] = o * o if h == 0 else squares[b] + o * o
    ones = jnp.ones((8, B), BF16)
    sub = iota((8, B), 0)
    sums = jnp.zeros((8, B), F32)
    for b in range(NB):
        hi, lo = split(squares[b])
        sums = jnp.where(sub == b, dot_nt(ones, hi) + dot_nt(ones, lo), sums)
    xsend_ref[...] = sums

    def send_x(i):
        return pltpu.make_async_remote_copy(
            src_ref=xsend_ref, dst_ref=xbuf_ref.at[i - 1],
            send_sem=x_send.at[i - 1], recv_sem=x_recv.at[i - 1],
            device_id={"head": lax.rem(head + i, 8)}, device_id_type=MESH,
        )

    for i in range(1, 8):
        send_x(i).start()
    for i in range(1, 8):
        send_x(i).wait()
        sums = sums + xbuf_ref[i - 1]
    scale = lax.rsqrt(sums / WIDTH + EPS)
    scale_ref[...] = jnp.concatenate([scale] * 16, 0).T
    for h in range(2):
        gain = gain_ref[:, h * B : h * B + B]
        for b in range(NB):
            rows = pl.ds(b * B, B)
            o_ref[rows, h * B : h * B + B] = (
                o1_ref[h, rows] * scale_ref[:, b : b + 1] * gain
            ).astype(BF16)

    for h in range(2):

        @pl.when(z != owner_z(h))
        def _():
            send_map(h, 0).wait_send()
            send_map(h, 1).wait_send()

    @pl.when(mine)
    def _():
        for i in range(1, ROWS):
            send_state(i).wait_send()

        @pl.when((y == 1) | (y == 2))
        def _():
            send_y(0, 0, 1).wait_send()

        @pl.when(y <= 2)
        def _():
            send_y(1, 1, 1).wait_send()

        @pl.when(y <= 1)
        def _():
            send_y(1, 2, 2).wait_send()


def local(queries, key_vectors, value_vectors, write_rates, doc_lengths, norm_gain):
    vm = pl.BlockSpec(memory_space=pltpu.VMEM)
    return pl.pallas_call(
        kernel,
        out_shape=pltpu.VMEM(queries.shape, BF16),
        in_specs=[pl.BlockSpec(memory_space=pltpu.SMEM)]
        + [pl.BlockSpec(memory_space=pltpu.HBM)] * 5,
        out_specs=vm,
        scratch_shapes=[
            pltpu.VMEM((NB * B, 2 * B), BF16),
            pltpu.VMEM((NB * B, 2 * B), BF16),
            pltpu.VMEM((NB * B, 2 * B), BF16),
            pltpu.VMEM((2, NB * B), F32),
            pltpu.VMEM((1, 2 * B), F32),
            pltpu.VMEM((B, B), F32),
            pltpu.VMEM((NB, B), F32),
            pltpu.VMEM((B, B), F32),
            pltpu.VMEM((2, NB, B, 2 * B), F32),
            pltpu.VMEM((2, 8, B, 2 * B), BF16),
            pltpu.VMEM((2, NB, B, B), F32),
            pltpu.VMEM((2, 2, B, B), F32),
            pltpu.VMEM((ROWS, 2, B, B), F32),
            pltpu.VMEM((3, B, B), F32),
            pltpu.VMEM((2, B, B), F32),
            pltpu.VMEM((ROWS, B, 2 * B), BF16),
            pltpu.VMEM((ROWS, B, B), F32),
            pltpu.VMEM((8, B, 2 * B), BF16),
            pltpu.VMEM((7, B, 2 * B), BF16),
            pltpu.VMEM((ROWS, B, B), F32),
            pltpu.VMEM((2, B, B), F32),
            pltpu.VMEM((2, NB * B, 2 * B), BF16),
            pltpu.VMEM((2, NB * B, B), F32),
            pltpu.VMEM((8, B), F32),
            pltpu.VMEM((7, 8, B), F32),
            pltpu.SemaphoreType.DMA((7,)),
            pltpu.SemaphoreType.DMA((2, 2)),
            pltpu.SemaphoreType.DMA((ROWS, 2)),
            pltpu.SemaphoreType.DMA((3,)),
            pltpu.SemaphoreType.DMA((3,)),
            pltpu.SemaphoreType.DMA((ROWS,)),
            pltpu.SemaphoreType.DMA((2,)),
            pltpu.SemaphoreType.DMA((7,)),
            pltpu.SemaphoreType.DMA((7,)),
        ],
        compiler_params=pltpu.CompilerParams(
            collective_id=0, has_side_effects=True, vmem_limit_bytes=63 << 20
        ),
    )(doc_lengths, queries, key_vectors, value_vectors, write_rates.T, norm_gain[None])


def solution(mesh):
    tokens = P("ctx", "head")
    return jax.shard_map(
        local, mesh=mesh, in_specs=(tokens,) * 4 + (P(), P("head")), out_specs=tokens,
        check_vma=False,
    )
```

```python
import functools

import jax
import jax.numpy as jnp
from jax import lax
from jax.experimental import pallas as pl
from jax.experimental.pallas import tpu as pltpu
from jax.sharding import PartitionSpec as P

MESH = pl.DeviceIdType.MESH
F32, BF16 = jnp.float32, jnp.bfloat16
EPS = 1e-6
B = 128
NB = 8
ROWS = 8
WIDTH = 2048


def dotf(a, b):
    return lax.dot_general(a, b, (((1,), (0,)), ((), ())), preferred_element_type=F32)


def dot_nt(a, b):
    return lax.dot_general(a, b, (((1,), (1,)), ((), ())), preferred_element_type=F32)


def dot_tn(a, b):
    return lax.dot_general(a, b, (((0,), (0,)), ((), ())), preferred_element_type=F32)


def split(x):
    hi = x.astype(BF16)
    return hi, (x - hi.astype(F32)).astype(BF16)


def dot3(a, b):
    (ah, al), (bh, bl) = a, b
    return dotf(jnp.concatenate([ah, al], 1), jnp.concatenate([bh, bh], 0)) + dotf(ah, bl)


def wide(x):
    return jnp.concatenate(split(x), 1)


def dotw(a, b):
    n = b.shape[1] // 2
    r = dotf(a, jnp.concatenate([b, b], 0))
    return r[:, :n] + r[:, n:]


def products(ms):
    w = [wide(m) for m in ms]
    m01, m23, m45, m67 = [dotw(w[i + 1], w[i]) for i in range(0, 8, 2)]
    w01, w23, w45, w67 = [wide(m) for m in (m01, m23, m45, m67)]
    m03, m47 = dotw(w23, w01), dotw(w67, w45)
    w03, w47 = wide(m03), wide(m47)
    total = dotw(w47, w03)
    w27 = wide(dotw(w47, w23))
    after = [dotw(w27, w[1]), None, dotw(w47, w[3]), None, dotw(w67, w[5])]
    after = [wide(after[0]), w27, wide(after[2]), w47, wide(after[4]), w67, w[7]]
    return total, after, (w, w01, w23, w45, w03)


def before(ws):
    w, w01, w23, w45, w03 = ws
    w6 = wide(dotw(w45, w03))
    return [w[0], w01, wide(dotw(w[2], w01)), w03, wide(dotw(w[4], w03)), w6, wide(dotw(w[6], w6))]


def added(a, get):
    a01 = dotw(get("1"), wide(a[0])) + a[1]
    a23 = dotw(get("3"), wide(a[2])) + a[3]
    a45 = dotw(get("5"), wide(a[4])) + a[5]
    w01 = wide(a01)
    a03 = dotw(get("23"), w01) + a23
    w03 = wide(a03)
    a6 = dotw(get("45"), w03) + a45
    return [
        a[0], a01, dotw(get("2"), w01) + a[2], a03, dotw(get("4"), w03) + a[4], a6,
        dotw(get("6"), wide(a6)) + a[6],
    ]


def total_added(after, a):
    t = a[7]
    for i in range(7):
        t = t + dotw(after[i], wide(a[i]))
    return t


NAMES = {"1": 0, "2": 1, "3": 2, "4": 3, "5": 4, "6": 5, "23": 6, "45": 7}


def keep_products(ref, ws):
    w, w01, w23, w45, w03 = ws
    for name, x in zip(NAMES, [w[1], w[2], w[3], w[4], w[5], w[6], w23, w45]):
        ref[NAMES[name]] = x


def iota(shape, dim):
    return lax.broadcasted_iota(jnp.int32, shape, dim)


SIZES = (8, 16, 32, 64)


def stack_parts(x):
    hi = x.astype(BF16).astype(F32)
    return jnp.concatenate([hi, x - hi], 0).astype(BF16)


def dot_stacked(a, b):
    m, n = a.shape[0] // 2, b.shape[1] // 2
    r = dotf(a, b)
    return r[:m, :n] + (r[m:, :n] + r[:m, n:])


def invert(lows):
    row, col = iota((B, B), 0), iota((B, B), 1)
    n = len(lows)
    near = (row // 8) == (col // 8)
    parts = [
        stack_parts(jnp.sum(jnp.where(near, low, 0.0).reshape(16, 8, B), axis=0)) for low in lows
    ]
    lsp = [jnp.concatenate(split(low), 1) for low in lows]
    stacked = jnp.concatenate(parts, 0)
    spread = []
    for m in range(7):
        pick = jnp.where(near & (row % 8 == m), 1.0, 0.0).astype(BF16)
        r = dotf(stacked, pick).reshape(n, 2, 8, B)
        spread.append(r[:, 0] + r[:, 1])
    inv = jnp.broadcast_to((iota((8, B), 1) % 8 == iota((8, B), 0)).astype(F32), (n, 8, B))
    for m in range(7):
        inv = inv - spread[m] * inv[:, m : m + 1]
    inv = [inv[s] for s in range(n)]
    row2, col2 = iota((B, 2 * B), 0), iota((B, 2 * B), 1) % B
    for size in SIZES:
        below = (row2 // size == col2 // size + 1) & (row2 // size % 2 == 1)
        same = row2 // size == col2 // size
        odd = iota((size, B), 1) // size % 2 == 1
        xs, tops = [], []
        for s in range(n):
            upper = jnp.where(odd, 0.0, inv[s])
            inv[s] = jnp.where(odd, inv[s], 0.0)
            tops.append(upper)
            low = jnp.where(below, lsp[s], jnp.zeros_like(lsp[s]))
            xs.append(dot_stacked(stack_parts(inv[s]), low))
        for s in range(n):
            two = [tops[s]] * (16 // size if size < 16 else 1)
            two = jnp.concatenate(two, 0) if len(two) > 1 else two[0]
            wide = jnp.concatenate(split(two), 1)
            wide = jnp.concatenate([wide] * (B // wide.shape[0]), 0)
            wide = jnp.where(same, wide, jnp.zeros_like(wide))
            y = dot_stacked(stack_parts(xs[s]), wide)
            inv[s] = jnp.concatenate([tops[s], inv[s] - y], 0)
    return inv


def kernel(
    doc_ref, q_hbm, k_hbm, v_hbm, rate_hbm, gain_hbm, o_ref,
    q_ref, k_ref, v_ref, rate_ref, gain_ref, cols_ref, end_ref, scale_ref, wu_ref, prod_ref, add_ref, mat_ref, got_ref, ybuf_ref, ysend_ref, pz_ref, pa_ref, oprod_ref, oafter_ref,
    sout_ref, sbuf_ref, qp_ref, o1_ref, xsend_ref, xbuf_ref,
    in_sem, g_send, g_recv, y_send, y_recv, s_send, s_recv, x_send, x_recv,
):
    def load(i, hbm, ref, h):
        if h is not None:
            hbm, ref = hbm.at[:, h * B : h * B + B], ref.at[:, h * B : h * B + B]
        return pltpu.make_async_copy(hbm, ref, in_sem.at[i])

    loads = [
        load(0, rate_hbm, rate_ref, None),
        load(1, k_hbm, k_ref, 0),
        load(2, v_hbm, v_ref, 0),
        load(3, k_hbm, k_ref, 1),
        load(4, v_hbm, v_ref, 1),
        load(5, gain_hbm, gain_ref, None),
        load(6, q_hbm, q_ref, None),
    ]
    for i in (1, 0, 3, 2, 4, 5, 6):
        loads[i].start()
    ctx, head = lax.axis_index("ctx"), lax.axis_index("head")
    y, z = ctx // ROWS, lax.rem(ctx, ROWS)
    core = lax.rem(head, 2)

    def at_z(other):
        return {"ctx": y * ROWS + other}

    def at_y(other):
        return {"ctx": lax.rem(other, 4) * ROWS + z}

    def owner_z(h):
        return 4 * core + 2 * h

    mine = (z // 4 == core) & (lax.rem(z, 2) == 0)
    my_h = lax.rem(z, 4) // 2

    barrier = pltpu.get_barrier_semaphore()
    for i in range(1, ROWS):
        pl.semaphore_signal(barrier, 1, device_id=at_z(lax.rem(z + i, ROWS)), device_id_type=MESH)
    for i in range(1, 4):
        pl.semaphore_signal(barrier, 1, device_id=at_y(y + i), device_id_type=MESH)
    for i in range(1, 8):
        pl.semaphore_signal(barrier, 1, device_id={"head": lax.rem(head + i, 8)}, device_id_type=MESH)

    base = ctx * (NB * B)
    pos = base + iota((NB, B), 0) * B + iota((NB, B), 1)
    begin = jnp.int32(0)
    start = jnp.zeros((NB, B), jnp.int32)
    end = jnp.full((NB, B), doc_ref[0])
    for m in range(31):
        begin = begin + doc_ref[m]
        passed = pos >= begin
        start = jnp.where(passed, begin, start)
        end = jnp.where(passed, begin + doc_ref[m + 1], end)
    end_ref[...] = (end - base - iota((NB, B), 0) * B).astype(F32)
    loads[0].wait()
    rates = [rate_ref[h : h + 1, b * B : b * B + B] for h in range(2) for b in range(NB)]
    start_f = (start - base).astype(F32)
    cols_ref[...] = jnp.concatenate([start_f] + rates + [start_f] * 13, 0).T

    row, col = iota((B, B), 0), iota((B, B), 1)
    eye = (row == col).astype(F32)
    rowf = row.astype(F32)
    ones2 = jnp.ones((2 * B, B), BF16)

    def same_doc(b):
        return rowf < end_ref[b : b + 1]

    def carried(b):
        return (cols_ref[:, b : b + 1] < float(b * B)).astype(F32)

    def unbroken(b):
        return (cols_ref[B - 1 : B, b : b + 1] < float(b * B)).astype(F32)

    def last_keys(b, kt):
        return jnp.where(end_ref[b : b + 1] >= float(B), kt.astype(F32), 0.0).astype(BF16)

    def norms(x):
        return lax.rsqrt(dotf(wide(x * x), ones2) + EPS)

    def lanes(h):
        return pl.ds(pl.multiple_of(h * B, B), B)

    def rate(b, h):
        i = NB + h * NB + b
        return cols_ref[:, i : i + 1]

    def own_product(h):
        lows, rights, scales = [], [], []
        for b in range(NB):
            kb = k_ref[pl.ds(b * B, B), lanes(h)]
            kf = kb.astype(F32)
            rk = norms(kf)
            keep = (row > col) & same_doc(b)
            scale = rate(b, h) * rk
            scales.append(scale)
            lows.append(jnp.where(keep, dot_nt(kb, kb) * (scale * rk), 0.0))
            rights.append(wide(kf * (scale * rk)))
        inv = [wide(t) for t in invert(lows)]
        ws = [dotw(inv[b], rights[b]) for b in range(NB)]
        ms, kts = [], []
        for b in range(NB):
            wu_ref[h, b, :, :B] = ws[b]
            kt = k_ref[pl.ds(b * B, B), lanes(h)].T
            m = dotf(jnp.concatenate([kt, kt], 1), jnp.concatenate(split(ws[b]), 0))
            ms.append((eye - m) * unbroken(b))
            kts.append(kt)
        total, after, some = products(ms)
        mat_ref[h, 0] = total
        return inv, scales, kts, after, some

    def own_added(h, inv, scales, kts, after):
        us = []
        for b in range(NB):
            vf = v_ref[pl.ds(b * B, B), lanes(h)].astype(F32)
            us.append(dotw(inv[b], wide(vf * scales[b])))
        adds = []
        for b in range(NB):
            wu_ref[h, b, :, B:] = us[b]
            kt = last_keys(b, kts[b])
            adds.append(dotf(jnp.concatenate([kt, kt], 1), jnp.concatenate(split(us[b]), 0)))
            add_ref[h, b] = adds[b]
        mat_ref[h, 1] = total_added(after, adds)

    def send_map(h, part):
        return pltpu.make_async_remote_copy(
            src_ref=mat_ref.at[h, part], dst_ref=got_ref.at[z, part],
            send_sem=g_send.at[h, part], recv_sem=g_recv.at[z, part],
            device_id=at_z(owner_z(h)), device_id_type=MESH,
        )

    def give(h, part):
        @pl.when(z != owner_z(h))
        def _():
            send_map(h, part).start()

        @pl.when(z == owner_z(h))
        def _():
            got_ref[z, part] = mat_ref[h, part]

    @pl.when(y < 2)
    def _():
        ybuf_ref[0] = jnp.zeros((B, B), F32)
        ybuf_ref[2] = jnp.zeros((B, B), F32)

    @pl.when(y == 0)
    def _():
        ybuf_ref[1] = jnp.zeros((B, B), F32)

    loads[1].wait()
    left = [own_product(0)]
    pl.semaphore_wait(barrier, 17)
    give(0, 0)
    loads[3].wait()
    left.append(own_product(1))
    give(1, 0)
    loads[2].wait()
    loads[4].wait()
    own_added(0, *left[0][:4])
    own_added(1, *left[1][:4])
    give(0, 1)
    give(1, 1)

    def shadow(h):
        keep_products(prod_ref.at[h], left[h][4])
        bms = before(left[h][4])
        adds = added([add_ref[h, b] for b in range(NB)], lambda name: prod_ref[h, NAMES[name]])
        scores, lefts = [], []
        for b in range(NB):
            kb = k_ref[pl.ds(b * B, B), lanes(h)]
            qb = q_ref[pl.ds(b * B, B), lanes(h)]
            qf = qb.astype(F32)
            rq = norms(qf)
            keep = (row >= col) & same_doc(b)
            scores.append(jnp.where(keep, dot_nt(qb, kb) * rq, 0.0))
            lefts.append(qf * rq)
        both = [dot3(split(scores[b]), split(wu_ref[h, b])) for b in range(NB)]
        qes = [(lefts[b] - both[b][:, :B]) * carried(b) for b in range(NB)]
        o1s = [both[b][:, B:] for b in range(NB)]
        qxs = []
        for b in range(1, NB):
            bm, (ah, al) = bms[b - 1], split(adds[b - 1])
            right = (
                jnp.concatenate([bm[:, :B], ah], 1),
                jnp.concatenate([bm[:, B:], al], 1),
            )
            qxs.append(dot3(split(qes[b]), right))
        for b in range(NB):
            qe, o1 = qes[b], o1s[b]
            if b > 0:
                qe, o1 = qxs[b - 1][:, :B], o1 + qxs[b - 1][:, B:]
            hi, lo = split(qe)
            qp_ref[h, pl.ds(b * B, B)] = jnp.concatenate([hi, lo], 1)
            o1_ref[h, pl.ds(b * B, B)] = o1

    loads[5].wait()
    loads[6].wait()
    shadow(0)
    def send_y(src, slot, step):
        return pltpu.make_async_remote_copy(
            src_ref=ysend_ref.at[src], dst_ref=ybuf_ref.at[slot],
            send_sem=y_send.at[slot], recv_sem=y_recv.at[slot],
            device_id=at_y(y + step), device_id_type=MESH,
        )

    def send_state(to):
        return pltpu.make_async_remote_copy(
            src_ref=sout_ref.at[to], dst_ref=sbuf_ref.at[my_h],
            send_sem=s_send.at[to], recv_sem=s_recv.at[my_h],
            device_id=at_z(to), device_id_type=MESH,
        )

    def wait_maps(part):
        for i in range(1, ROWS):
            frm = lax.rem(z + i, ROWS)
            pltpu.make_async_remote_copy(
                src_ref=mat_ref.at[0, part], dst_ref=got_ref.at[frm, part],
                send_sem=g_send.at[0, part], recv_sem=g_recv.at[frm, part],
                device_id=at_z(frm), device_id_type=MESH,
            ).wait_recv()

    @pl.when(mine)
    def _():
        wait_maps(0)
        total, after, some = products([got_ref[i, 0] for i in range(ROWS)])
        ysend_ref[0] = total
        @pl.when((y == 1) | (y == 2))
        def _():
            send_y(0, 0, 1).start()

        keep_products(oprod_ref, some)
        pz_ref[0] = jnp.concatenate([eye, jnp.zeros_like(eye)], 1).astype(BF16)
        for i, x in enumerate(before(some)):
            pz_ref[i + 1] = x
        for i, x in enumerate(after):
            oafter_ref[i] = x
        wait_maps(1)
        states = [got_ref[i, 1] for i in range(ROWS)]
        ysend_ref[1] = total_added([oafter_ref[i] for i in range(7)], states)
        @pl.when(y <= 2)
        def _():
            send_y(1, 1, 1).start()

        @pl.when(y <= 1)
        def _():
            send_y(1, 2, 2).start()

    shadow(1)

    @pl.when(mine)
    def _():
        states = [got_ref[i, 1] for i in range(ROWS)]
        pa_ref[0] = jnp.zeros((B, B), F32)
        for i, x in enumerate(added(states, lambda name: oprod_ref[NAMES[name]])):
            pa_ref[i + 1] = x
        @pl.when(y >= 1)
        def _():
            send_y(1, 1, 1).wait_recv()

        @pl.when(y >= 2)
        def _():
            send_y(0, 0, 1).wait_recv()
            send_y(1, 2, 2).wait_recv()

        s_row = ybuf_ref[1] + dotw(wide(ybuf_ref[0]), wide(ybuf_ref[2]))
        sh, sl = split(s_row)
        shh = jnp.concatenate([sh, sh], 0)
        for to in (1, 2, 0, 3, 4, 7, 6, 5):
            pm = pz_ref[to]
            sout_ref[to] = pa_ref[to] + dotf(pm, shh) + dotf(pm[:, :B], sl)

            @pl.when(z != to)
            def _():
                send_state(to).start()

        sbuf_ref[my_h] = sout_ref[z]

    for h in range(2):

        @pl.when(z != owner_z(h))
        def _():
            pltpu.make_async_remote_copy(
                src_ref=sout_ref.at[0], dst_ref=sbuf_ref.at[h],
                send_sem=s_send.at[0], recv_sem=s_recv.at[h],
                device_id=at_z(owner_z(h)), device_id_type=MESH,
            ).wait_recv()

    squares = [None] * NB
    for h in range(2):
        sh, sl = split(sbuf_ref[h])
        shh = jnp.concatenate([sh, sh], 0)
        for b in range(NB):
            rows = pl.ds(b * B, B)
            qp = qp_ref[h, rows]
            o = o1_ref[h, rows] + dotf(qp, shh) + dotf(qp[:, :B], sl)
            o1_ref[h, rows] = o
            squares[b] = o * o if h == 0 else squares[b] + o * o
    ones = jnp.ones((8, B), BF16)
    sub = iota((8, B), 0)
    sums = jnp.zeros((8, B), F32)
    for b in range(NB):
        hi, lo = split(squares[b])
        sums = jnp.where(sub == b, dot_nt(ones, hi) + dot_nt(ones, lo), sums)
    xsend_ref[...] = sums

    def send_x(i):
        return pltpu.make_async_remote_copy(
            src_ref=xsend_ref, dst_ref=xbuf_ref.at[i - 1],
            send_sem=x_send.at[i - 1], recv_sem=x_recv.at[i - 1],
            device_id={"head": lax.rem(head + i, 8)}, device_id_type=MESH,
        )

    for i in range(1, 8):
        send_x(i).start()
    for i in range(1, 8):
        send_x(i).wait()
        sums = sums + xbuf_ref[i - 1]
    scale = lax.rsqrt(sums / WIDTH + EPS)
    scale_ref[...] = jnp.concatenate([scale] * 16, 0).T
    for h in range(2):
        gain = gain_ref[:, h * B : h * B + B]
        for b in range(NB):
            rows = pl.ds(b * B, B)
            o_ref[rows, h * B : h * B + B] = (
                o1_ref[h, rows] * scale_ref[:, b : b + 1] * gain
            ).astype(BF16)

    for h in range(2):

        @pl.when(z != owner_z(h))
        def _():
            send_map(h, 0).wait_send()
            send_map(h, 1).wait_send()

    @pl.when(mine)
    def _():
        for i in range(1, ROWS):
            send_state(lax.rem(z + i, ROWS)).wait_send()

        @pl.when((y == 1) | (y == 2))
        def _():
            send_y(0, 0, 1).wait_send()

        @pl.when(y <= 2)
        def _():
            send_y(1, 1, 1).wait_send()

        @pl.when(y <= 1)
        def _():
            send_y(1, 2, 2).wait_send()


def local(queries, key_vectors, value_vectors, write_rates, doc_lengths, norm_gain):
    vm = pl.BlockSpec(memory_space=pltpu.VMEM)
    return pl.pallas_call(
        kernel,
        out_shape=pltpu.VMEM(queries.shape, BF16),
        in_specs=[pl.BlockSpec(memory_space=pltpu.SMEM)]
        + [pl.BlockSpec(memory_space=pltpu.HBM)] * 5,
        out_specs=vm,
        scratch_shapes=[
            pltpu.VMEM((NB * B, 2 * B), BF16),
            pltpu.VMEM((NB * B, 2 * B), BF16),
            pltpu.VMEM((NB * B, 2 * B), BF16),
            pltpu.VMEM((2, NB * B), F32),
            pltpu.VMEM((1, 2 * B), F32),
            pltpu.VMEM((B, B), F32),
            pltpu.VMEM((NB, B), F32),
            pltpu.VMEM((B, B), F32),
            pltpu.VMEM((2, NB, B, 2 * B), F32),
            pltpu.VMEM((2, 8, B, 2 * B), BF16),
            pltpu.VMEM((2, NB, B, B), F32),
            pltpu.VMEM((2, 2, B, B), F32),
            pltpu.VMEM((ROWS, 2, B, B), F32),
            pltpu.VMEM((3, B, B), F32),
            pltpu.VMEM((2, B, B), F32),
            pltpu.VMEM((ROWS, B, 2 * B), BF16),
            pltpu.VMEM((ROWS, B, B), F32),
            pltpu.VMEM((8, B, 2 * B), BF16),
            pltpu.VMEM((7, B, 2 * B), BF16),
            pltpu.VMEM((ROWS, B, B), F32),
            pltpu.VMEM((2, B, B), F32),
            pltpu.VMEM((2, NB * B, 2 * B), BF16),
            pltpu.VMEM((2, NB * B, B), F32),
            pltpu.VMEM((8, B), F32),
            pltpu.VMEM((7, 8, B), F32),
            pltpu.SemaphoreType.DMA((7,)),
            pltpu.SemaphoreType.DMA((2, 2)),
            pltpu.SemaphoreType.DMA((ROWS, 2)),
            pltpu.SemaphoreType.DMA((3,)),
            pltpu.SemaphoreType.DMA((3,)),
            pltpu.SemaphoreType.DMA((ROWS,)),
            pltpu.SemaphoreType.DMA((2,)),
            pltpu.SemaphoreType.DMA((7,)),
            pltpu.SemaphoreType.DMA((7,)),
        ],
        compiler_params=pltpu.CompilerParams(
            collective_id=0, has_side_effects=True, vmem_limit_bytes=63 << 20
        ),
    )(doc_lengths, queries, key_vectors, value_vectors, write_rates.T, norm_gain[None])


def solution(mesh):
    tokens = P("ctx", "head")
    return jax.shard_map(
        local, mesh=mesh, in_specs=(tokens,) * 4 + (P(), P("head")), out_specs=tokens,
        check_vma=False,
    )
```
